256 devices in a mesh: dp: 256 (over y, z, x, core).
Axes of the slice: x: 4, y: 4, z: 8, core: 2. Of those that a mesh axis runs over, the one named last changes fastest.
Arguments:
- image_feat: bfloat16 [131072, 1152], P('dp'), may hold values from -6 to 6
- text_feat: bfloat16 [131072, 1152], P('dp'), may hold values from -6 to 6
- image_proj: bfloat16 [1152, 1152], replicated, may hold values from -0.1875 to 0.1875
- text_proj: bfloat16 [1152, 1152], replicated, may hold values from -0.1875 to 0.1875
- logit_scale_logarithm: float32 [1], replicated, may hold values from 0 to 1.5
- bias: float32 [1], replicated, may hold values from -2 to 0
- counts: int32 [256], P('dp'), may hold values from 1 to 4, 512 in all
Outputs:
- image_proj_grad: float32 [1327104], P('dp')
- text_proj_grad: float32 [1327104], P('dp')
The draws below stay inside these ranges and needn't reach their ends.
Inputs may be any that keep to these rules, and one draw needn't show every extreme that they name: counts holds whole pair blocks of 128 pairs; the counts sum to 512, and at least one device holds 4 blocks.
All inputs are finite; a program needn't handle non-finite values.
Results may differ from the reference program's by a relative error of at most 0.0043.
Values may be sent and summed in bfloat16 or wider, within the bound.
No kernel may reach another device: no remote copies, remote signals or barrier semaphores. Data moves between devices by JAX's collectives and lax.ppermute only.
A program may use at most 128 MiB of HBM per device.

```python
import math
import jax
import jax.numpy as jnp
import numpy as np
from jax import lax

D = 1152
BLK = 128
MAXB = 4
STEPS = 4
CAP = 512
ROWS = 131072
N_DP = 256


def shard_levels(key, dims, split, low, high):
    def one(position, parts):
        draws = jax.random.uniform(jax.random.fold_in(jax.random.fold_in(key, 6), position), (parts,), jnp.float32, low / len(split), high / len(split))
        return jnp.repeat(jnp.exp(draws), dims[position] // parts).reshape((-1,) + (1,) * (len(dims) - position - 1))

    factor_of = one(*split[0])
    for cut in split[1:]:
        factor_of = factor_of * one(*cut)
    return factor_of


def length_profile(count, total, reach, lean):
    portions = [(1 << 20) // math.isqrt(rank ** lean) + 1 for rank in range(2, count + 1)]
    surplus, given = total - reach - (count - 1), [1] * (count - 1)
    while surplus > 0:
        free = [i for i in range(count - 1) if given[i] < reach]
        whole, left = sum([portions[i] for i in free]), surplus
        for i in free:
            more = min(reach - given[i], max(1, left * portions[i] // whole), surplus)
            given[i] = given[i] + more
            surplus = surplus - more
    return np.array([reach] + given)


def ragged(rng, number_of, total, bound, slope):
    if number_of == 2:
        one = jax.random.randint(rng, (), max(1, total - bound), min(bound, total - 1) + 1)
        return jnp.stack([one, total - one])
    tallies = jnp.asarray(length_profile(number_of, total, bound, slope), jnp.int32)
    couples = (number_of - 1) // 2
    source_of, receiver = tallies[1:1 + 2 * couples:2], tallies[2:2 + 2 * couples:2]
    room = jnp.minimum(source_of - 1, bound - receiver)
    moved = jax.random.randint(jax.random.fold_in(rng, 1), (couples,), 0, 1 << 20) % (room + 1)
    tallies = tallies.at[1:1 + 2 * couples:2].set(source_of - moved).at[2:2 + 2 * couples:2].set(receiver + moved)
    return tallies[jax.random.permutation(jax.random.fold_in(rng, 2), number_of)]


def bell_draw(own_key, extent, spread, bound, cuts=(), kind=jnp.bfloat16):
    result = jax.random.normal(own_key, extent, jnp.float32) * spread
    if len(cuts) > 0:
        result = shard_levels(own_key, extent, cuts, -0.22, 0.18) * result
    return jnp.clip(result, min=-bound, max=bound).astype(kind)


def setup_inputs(seed: int = 0) -> dict:
    arg_keys = jax.random.split(jax.random.key(seed), 8)
    image_feat = bell_draw(arg_keys[0], (ROWS, D), 1.0, 6.0, ((0, 256),))
    text_feat = bell_draw(arg_keys[1], (ROWS, D), 1.0, 6.0, ((0, 256),))
    image_proj = bell_draw(arg_keys[2], (D, D), D ** -0.5, 0.1875)
    text_proj = bell_draw(arg_keys[3], (D, D), D ** -0.5, 0.1875)
    logit_scale_logarithm = jnp.clip(jax.random.uniform(arg_keys[4], (1,), jnp.float32, 0.0, 1.5), 0.0, 1.5)
    bias = jnp.clip(jax.random.uniform(arg_keys[5], (1,), jnp.float32, -2.0, 0.0), -2.0, 0.0)
    counts = ragged(arg_keys[6], N_DP, 2 * N_DP, MAXB, 1).astype(jnp.int32)
    return {"image_feat": image_feat, "text_feat": text_feat, "image_proj": image_proj, "text_proj": text_proj, "logit_scale_logarithm": logit_scale_logarithm, "bias": bias, "counts": counts}


def project_rows(features, weight_tensors):
    projected = jnp.dot(features, weight_tensors, preferred_element_type=jnp.float32)
    row_norm = jnp.sqrt(lax.optimization_barrier(jnp.sum(projected * projected, axis=1, keepdims=True)) + 1e-06)
    return (projected / row_norm, row_norm)

def raw_grad(gradient, direction, row_norm):
    radial = lax.optimization_barrier(jnp.sum(direction * gradient, axis=1, keepdims=True))
    return ((gradient - direction * radial) / row_norm).astype(jnp.bfloat16)

def reference(image_feat, text_feat, image_proj, text_proj, logit_scale_logarithm, bias, counts):
    softness_factor = jnp.exp(logit_scale_logarithm[0])
    shard_displacement = bias[0]
    image_dir, image_norm = project_rows(image_feat, image_proj)
    text_dir, text_norm = project_rows(text_feat, text_proj)
    picture_unit_vector = lax.optimization_barrier(image_dir.astype(jnp.bfloat16)).astype(jnp.float32).reshape(N_DP, CAP, D)
    caption_unit_vector = lax.optimization_barrier(text_dir.astype(jnp.bfloat16)).astype(jnp.float32).reshape(N_DP, CAP, D)
    row_index = jnp.arange(CAP, dtype=jnp.int32)
    live = row_index[None, :] < counts[:, None] * BLK
    positive = row_index[:, None] == row_index[None, :]
    picture_gradient = jnp.zeros((N_DP, CAP, D), jnp.float32)
    text_grad = jnp.zeros((N_DP, CAP, D), jnp.float32)
    for cycle_step in range(STEPS):
        incoming_shard = jnp.roll(caption_unit_vector, cycle_step, axis=0)
        visiting_live = jnp.roll(live, cycle_step, axis=0)
        cosine_affinity = jnp.einsum('nad,ncd->nac', picture_unit_vector, incoming_shard)
        pair_logit_matrix = softness_factor * cosine_affinity + shard_displacement
        if cycle_step == 0:
            pairing_weight = jnp.where(positive[None], -jax.nn.sigmoid(-pair_logit_matrix), jax.nn.sigmoid(pair_logit_matrix))
        else:
            pairing_weight = jax.nn.sigmoid(pair_logit_matrix)
        pairing_weight = jnp.where(live[:, :, None] & visiting_live[:, None, :], pairing_weight, 0.0)
        pairing_weight = lax.optimization_barrier(pairing_weight.astype(jnp.bfloat16)).astype(jnp.float32)
        picture_gradient = picture_gradient + softness_factor * jnp.einsum('wfp,wpv->wfv', pairing_weight, incoming_shard)
        caption_contribution = softness_factor * jnp.einsum('uqv,uqh->uvh', pairing_weight, picture_unit_vector)
        text_grad = text_grad + jnp.roll(caption_contribution, -cycle_step, axis=0)
    image_delta = raw_grad(picture_gradient.reshape(-1, D), image_dir, image_norm)
    text_delta = raw_grad(text_grad.reshape(-1, D), text_dir, text_norm)
    image_weight_grad = jnp.dot(image_feat.T, image_delta, preferred_element_type=jnp.float32)
    text_weight_grad = jnp.dot(text_feat.T, text_delta, preferred_element_type=jnp.float32)
    return (image_weight_grad.reshape(-1), text_weight_grad.reshape(-1))
```

```python
import jax
import jax.numpy as jnp
from jax import lax
from jax.sharding import PartitionSpec as P

BLK = 128
D = 1152
NY, NZ, NX = 4, 8, 4
N = 256
BF = jnp.bfloat16
F32 = jnp.float32


def dev(y, z, x, c):
    return ((y * NZ + z) * NX + x) * 2 + c


PLANES = [
    [dev(y, z, x, c) for y in range(NY) for x in range(NX)]
    for z in range(NZ)
    for c in range(2)
]
COLUMNS = [
    [dev(y, z, x, c) for z in range(NZ)]
    for y in range(NY)
    for x in range(NX)
    for c in range(2)
]
SWAP = [(d, d ^ 1) for d in range(N)]


def shift(value, steps):
    return lax.ppermute(value, "dp", [(d, (d + steps) % N) for d in range(N)])


def mm(a, b):
    return jnp.dot(a, b, preferred_element_type=F32)


def mm_t(a, b):
    return lax.dot_general(a, b, (((1,), (1,)), ((), ())), preferred_element_type=F32)


def t_mm(a, b):
    return lax.dot_general(a, b, (((0,), (0,)), ((), ())), preferred_element_type=F32)


def project_rows(features, proj):
    projected = mm(features, proj)
    norm = jnp.sqrt(jnp.sum(projected * projected, axis=1, keepdims=True) + 1e-06)
    return projected / norm, norm


def raw_grad(gradient, direction, norm):
    radial = jnp.sum(direction * gradient, axis=1, keepdims=True)
    return ((gradient - direction * radial) / norm).astype(BF)


def pair_weight(image_unit, text_unit, scale, bias, matches):
    logit = scale * mm_t(image_unit, text_unit) + bias
    if matches:
        rows = lax.broadcasted_iota(jnp.int32, logit.shape, 0)
        cols = lax.broadcasted_iota(jnp.int32, logit.shape, 1)
        weight = jnp.where(rows == cols, -jax.nn.sigmoid(-logit), jax.nn.sigmoid(logit))
    else:
        weight = jax.nn.sigmoid(logit)
    return weight.astype(BF)


def local(image_feat, text_feat, image_proj, text_proj, logit_scale_logarithm, bias, counts):
    scale = jnp.exp(logit_scale_logarithm[0])
    offset = bias[0]
    rows = lax.broadcasted_iota(jnp.int32, image_feat.shape, 0)
    live = rows < counts[0] * BLK
    zero = jnp.zeros((), BF)
    text0 = jnp.where(live, text_feat, zero)
    image0 = jnp.where(live, image_feat, zero)
    text2 = shift(text0, 2)
    image1 = shift(image0, -1)

    dir_i0, n_i0 = project_rows(image0, image_proj)
    dir_t0, n_t0 = project_rows(text0, text_proj)
    u_i0, u_t0 = dir_i0.astype(BF), dir_t0.astype(BF)
    w = pair_weight(u_i0, u_t0, scale, offset, True)
    g_i0 = mm(w, u_t0)
    g_t0 = t_mm(w, u_i0)

    dir_i1, n_i1 = project_rows(image1, image_proj)
    u_i1 = dir_i1.astype(BF)
    w = pair_weight(u_i1, u_t0, scale, offset, False)
    g_i1 = mm(w, u_t0)
    g_t0 = g_t0 + t_mm(w, u_i1)
    d_t0 = raw_grad(scale * g_t0, dir_t0, n_t0)
    term_t = t_mm(text0, d_t0)

    dir_t2, n_t2 = project_rows(text2, text_proj)
    u_t2 = dir_t2.astype(BF)
    w0 = pair_weight(u_i0, u_t2, scale, offset, False)
    w1 = pair_weight(u_i1, u_t2, scale, offset, False)
    g_i0 = g_i0 + mm(w0, u_t2)
    g_i1 = g_i1 + mm(w1, u_t2)
    g_t2 = t_mm(w0, u_i0) + t_mm(w1, u_i1)
    term_t = term_t + t_mm(text2, raw_grad(scale * g_t2, dir_t2, n_t2))
    term_i = t_mm(image0, raw_grad(scale * g_i0, dir_i0, n_i0)) + t_mm(
        image1, raw_grad(scale * g_i1, dir_i1, n_i1)
    )

    core = lax.axis_index("dp") % 2
    first = core == 0
    away = jnp.where(first, term_t, term_i).astype(BF)
    kept = jnp.where(first, term_i, term_t)
    chip = (kept + lax.ppermute(away, "dp", SWAP).astype(F32)).astype(BF)
    chip = chip.reshape(NY, NZ, NX, 9, D).transpose(0, 2, 1, 3, 4).reshape(16, 72, D)
    plane = lax.all_to_all(chip, "dp", 0, 0, axis_index_groups=PLANES, tiled=True)
    plane = jnp.sum(plane.astype(F32), axis=0).astype(BF).reshape(NZ, 9, D)
    column = lax.all_to_all(plane, "dp", 0, 0, axis_index_groups=COLUMNS, tiled=True)
    total = jnp.sum(column.astype(F32), axis=0).reshape(2, 9 * D // 2)
    mine = lax.dynamic_index_in_dim(total, core, 0, False)
    other = lax.ppermute(lax.dynamic_index_in_dim(total, 1 - core, 0, False), "dp", SWAP)
    return jnp.where(first, mine, other), jnp.where(first, other, mine)


def solution(mesh):
    return jax.shard_map(
        local,
        mesh=mesh,
        in_specs=(P("dp", None), P("dp", None), P(), P(), P(), P(), P("dp")),
        out_specs=(P("dp"), P("dp")),
        check_vma=False,
    )
```

```python
import functools

import jax
import jax.numpy as jnp
import numpy as np
from jax import lax
from jax.experimental import pallas as pl
from jax.experimental.pallas import tpu as pltpu
from jax.sharding import PartitionSpec as P

BLK = 128
D = 1152
R = 512
NY, NZ, NX = 4, 8, 4
N = 256
OWN = 9
COLS = 384
ROWS = 256
BF = jnp.bfloat16
F32 = jnp.float32
VMEM = pl.BlockSpec(memory_space=pltpu.VMEM)
SMEM = pl.BlockSpec(memory_space=pltpu.SMEM)


def dev(y, z, x, c):
    return ((y * NZ + z) * NX + x) * 2 + c


PLANES = [
    [dev(y, z, x, c) for y in range(NY) for x in range(NX)]
    for z in range(NZ)
    for c in range(2)
]
COLUMNS = [
    [dev(y, z, x, c) for z in range(NZ)]
    for y in range(NY)
    for x in range(NX)
    for c in range(2)
]
SWAP = [(d, d ^ 1) for d in range(N)]


def shuffle_matrix():
    flat = np.arange(D).reshape(NY, NZ, NX, OWN)
    source = flat.transpose(0, 2, 1, 3).reshape(-1)
    matrix = np.zeros((D, D), np.float32)
    matrix[np.arange(D), source] = 1.0
    return jnp.asarray(matrix, BF)


def shift(value, steps):
    return lax.ppermute(value, "dp", [(d, (d + steps) % N) for d in range(N)])


def mm(a, b):
    return jnp.dot(a, b, preferred_element_type=F32)


def mm_t(a, b):
    return lax.dot_general(a, b, (((1,), (1,)), ((), ())), preferred_element_type=F32)


def t_mm(a, b):
    return lax.dot_general(a, b, (((0,), (0,)), ((), ())), preferred_element_type=F32)


def cols(j):
    return pl.ds(pl.multiple_of(j * COLS, 128), COLS)


def project(feat_ref, proj_ref, dir_ref, unit_ref, inv_ref):
    def product(j, squares):
        raw = mm(feat_ref[...], proj_ref[:, cols(j)])
        dir_ref[:, cols(j)] = raw
        return squares + jnp.sum(raw * raw, axis=1, keepdims=True)

    squares = lax.fori_loop(0, D // COLS, product, jnp.zeros((R, 1), F32))
    inv_ref[...] = 1.0 / jnp.sqrt(squares + 1e-06)

    @pl.loop(0, R // ROWS)
    def _(i):
        rows = pl.ds(pl.multiple_of(i * ROWS, ROWS), ROWS)
        direction = dir_ref[rows, :] * inv_ref[rows, :]
        dir_ref[rows, :] = direction
        unit_ref[rows, :] = direction.astype(BF)


def turned(feat_ref, shuffle_ref, out_ref):
    @pl.loop(0, D // COLS)
    def _(j):
        rows = pl.ds(pl.multiple_of(j * COLS, COLS), COLS)
        out_ref[rows, :] = mm_t(shuffle_ref[rows, :], feat_ref[...]).astype(BF)


def raw_grad(gradient, direction, inverse):
    radial = jnp.sum(direction * gradient, axis=1, keepdims=True)
    return ((gradient - direction * radial) * inverse).astype(BF)


def weights(image_unit, text_unit, scale, bias):
    return scale * mm_t(image_unit, text_unit) + bias


def first_kernel(text, image, text_proj, image_proj, shuffle,
                 dir_t, unit_t, inv_t, turn_t, dir_i, unit_i, inv_i, turn_i):
    project(text, text_proj, dir_t, unit_t, inv_t)
    project(image, image_proj, dir_i, unit_i, inv_i)
    turned(text, shuffle, turn_t)
    turned(image, shuffle, turn_i)


def text_side(pair_ref, unit_i0, unit_i1, dir_t, inv_t, out_ref, scratch, scale):
    @pl.loop(0, D // COLS)
    def _(j):
        scratch[:, cols(j)] = scale * (
            t_mm(pair_ref[:R, :], unit_i0[:, cols(j)])
            + t_mm(pair_ref[R:, :], unit_i1[:, cols(j)])
        )

    @pl.loop(0, R // ROWS)
    def _(i):
        rows = pl.ds(pl.multiple_of(i * ROWS, ROWS), ROWS)
        out_ref[rows, :] = raw_grad(scratch[rows, :], dir_t[rows, :], inv_t[rows, :])


def second_kernel(scal, image1, image_proj, shuffle, unit_i0, unit_t0, dir_t0, inv_t0,
                  dir_i1, unit_i1, inv_i1, turn_i1, grad_i, delta_t0, pair, scratch):
    scale, bias = scal[0], scal[1]
    project(image1, image_proj, dir_i1, unit_i1, inv_i1)

    @pl.loop(0, R // ROWS)
    def _(i):
        rows = pl.ds(pl.multiple_of(i * ROWS, ROWS), ROWS)
        logit = weights(unit_i0[rows, :], unit_t0[...], scale, bias)
        at = lax.broadcasted_iota(jnp.int32, logit.shape, 0) + i * ROWS
        sign = jnp.where(at == lax.broadcasted_iota(jnp.int32, logit.shape, 1), -1.0, 1.0)
        weight = (sign * jax.nn.sigmoid(sign * logit)).astype(BF)
        pair[rows, :] = weight
        grad_i[rows, :] = mm(weight, unit_t0[...])

    @pl.loop(0, R // ROWS)
    def _(i):
        rows = pl.ds(pl.multiple_of(i * ROWS, ROWS), ROWS)
        below = pl.ds(pl.multiple_of(R + i * ROWS, ROWS), ROWS)
        weight = jax.nn.sigmoid(weights(unit_i1[rows, :], unit_t0[...], scale, bias)).astype(BF)
        pair[below, :] = weight
        grad_i[below, :] = mm(weight, unit_t0[...])

    text_side(pair, unit_i0, unit_i1, dir_t0, inv_t0, delta_t0, scratch, scale)
    turned(image1, shuffle, turn_i1)


def third_kernel(scal, text2, text_proj, shuffle, unit_i0, unit_i1, dir_i0, dir_i1, inv_i0, inv_i1,
                 grad_i, delta_i, delta_t2, turn_t2, dir_t2, unit_t2, inv_t2, pair, scratch):
    scale, bias = scal[0], scal[1]
    project(text2, text_proj, dir_t2, unit_t2, inv_t2)
    for unit_i, dir_i, inv_i, base in (
        (unit_i0, dir_i0, inv_i0, 0),
        (unit_i1, dir_i1, inv_i1, R),
    ):
        @pl.loop(0, R // ROWS)
        def _(i):
            rows = pl.ds(pl.multiple_of(i * ROWS, ROWS), ROWS)
            below = pl.ds(pl.multiple_of(base + i * ROWS, ROWS), ROWS)
            weight = jax.nn.sigmoid(weights(unit_i[rows, :], unit_t2[...], scale, bias)).astype(BF)
            pair[below, :] = weight
            gradient = scale * (grad_i[below, :] + mm(weight, unit_t2[...]))
            delta_i[below, :] = raw_grad(gradient, dir_i[rows, :], inv_i[rows, :])

    text_side(pair, unit_i0, unit_i1, dir_t2, inv_t2, delta_t2, scratch, scale)
    turned(text2, shuffle, turn_t2)


def term_kernel(image_row, which, turn_i0, turn_i1, delta_i, turn_t0, turn_t2, delta_t0, delta_t2, out):
    def total(turn_a, turn_b, delta_a, delta_b):
        @pl.loop(0, D // COLS)
        def _(j):
            out[:, cols(j)] = (
                mm(turn_a[...], delta_a[:, cols(j)]) + mm(turn_b[...], delta_b[:, cols(j)])
            ).astype(out.dtype)

    @pl.when(which[0] == image_row)
    def _():
        total(turn_i0, turn_i1, delta_i.at[:R], delta_i.at[R:])

    @pl.when(which[0] != image_row)
    def _():
        total(turn_t0, turn_t2, delta_t0, delta_t2)


def call(kernel, operands, outs, scratch=(), flops=0, name=None):
    shapes = [jax.ShapeDtypeStruct(shape, kind) for shape, kind in outs]
    moved = sum(a.size * a.dtype.itemsize for a in operands)
    moved += sum(int(np.prod(s.shape)) * s.dtype.itemsize for s in shapes)
    return pl.pallas_call(
        kernel,
        out_shape=shapes,
        in_specs=[SMEM if a.size < 8 else VMEM for a in operands],
        out_specs=[VMEM] * len(shapes),
        scratch_shapes=[pltpu.VMEM(shape, kind) for shape, kind in scratch],
        compiler_params=pltpu.CompilerParams(vmem_limit_bytes=40 << 20),
        cost_estimate=pl.CostEstimate(flops=flops, bytes_accessed=moved, transcendentals=0),
        name=name,
    )(*operands)


def local(image_feat, text_feat, image_proj, text_proj, logit_scale_logarithm, bias, counts):
    scal = jnp.stack([jnp.exp(logit_scale_logarithm[0]), bias[0]])
    rows = lax.broadcasted_iota(jnp.int32, image_feat.shape, 0)
    live = rows < counts[0] * BLK
    zero = jnp.zeros((), BF)
    text0 = jnp.where(live, text_feat, zero)
    image_feat, text0 = lax.optimization_barrier((image_feat, text0))
    image0 = jnp.where(live, image_feat, zero)
    text2 = shift(text0, 2)
    image1 = shift(image0, -1)
    shuffle = shuffle_matrix()

    unit, wide, line, turn = ((R, D), BF), ((R, D), F32), ((R, 1), F32), ((D, R), BF)
    step = 2 * R * D * D
    dir_t0, unit_t0, inv_t0, turn_t0, dir_i0, unit_i0, inv_i0, turn_i0 = call(
        first_kernel,
        (text0, image0, text_proj, image_proj, shuffle),
        [wide, unit, line, turn] * 2,
        flops=4 * step,
        name="own_rows",
    )
    dir_i1, unit_i1, inv_i1, turn_i1, grad_i, delta_t0 = call(
        second_kernel,
        (scal, image1, image_proj, shuffle, unit_i0, unit_t0, dir_t0, inv_t0),
        [wide, unit, line, turn, ((2 * R, D), F32), unit],
        [((2 * R, R), BF), ((R, D), F32)],
        flops=5 * step,
        name="own_texts",
    )
    delta_i, delta_t2, turn_t2 = call(
        third_kernel,
        (scal, text2, text_proj, shuffle, unit_i0, unit_i1, dir_i0, dir_i1, inv_i0, inv_i1, grad_i),
        [((2 * R, D), BF), unit, turn],
        [wide, unit, line, ((2 * R, R), BF), wide],
        flops=5 * step,
        name="far_texts",
    )

    core = lax.axis_index("dp") % 2
    which = core.reshape(1)
    terms = (which, turn_i0, turn_i1, delta_i, turn_t0, turn_t2, delta_t0, delta_t2)
    (away,) = call(functools.partial(term_kernel, 1), terms, [((D, D), BF)], flops=2 * step, name="away")
    back = lax.ppermute(away, "dp", SWAP)
    (kept,) = call(functools.partial(term_kernel, 0), terms, [((D, D), F32)], flops=2 * step, name="kept")
    chip = (kept + back.astype(F32)).astype(BF).reshape(NY * NX, NZ * OWN, D)
    plane = lax.all_to_all(chip, "dp", 0, 0, axis_index_groups=PLANES, tiled=True)
    plane = jnp.sum(plane.astype(F32), axis=0).astype(BF).reshape(NZ, OWN, D)
    column = lax.all_to_all(plane, "dp", 0, 0, axis_index_groups=COLUMNS, tiled=True)
    total = jnp.sum(column.astype(F32), axis=0).reshape(2, OWN * D // 2)
    first = core == 0
    mine = lax.dynamic_index_in_dim(total, core, 0, False)
    other = lax.ppermute(lax.dynamic_index_in_dim(total, 1 - core, 0, False), "dp", SWAP)
    return jnp.where(first, mine, other), jnp.where(first, other, mine)


def solution(mesh):
    return jax.shard_map(
        local,
        mesh=mesh,
        in_specs=(P("dp", None), P("dp", None), P(), P(), P(), P(), P("dp")),
        out_specs=(P("dp"), P("dp")),
        check_vma=False,
    )
```

```python
import functools

import jax
import jax.numpy as jnp
import numpy as np
from jax import lax
from jax.experimental import pallas as pl
from jax.experimental.pallas import tpu as pltpu
from jax.sharding import PartitionSpec as P

BLK = 128
D = 1152
R = 512
NY, NZ, NX = 4, 8, 4
N = 256
OWN = 9
HALF = 640
BF = jnp.bfloat16
F32 = jnp.float32
VMEM = pl.BlockSpec(memory_space=pltpu.VMEM)
SMEM = pl.BlockSpec(memory_space=pltpu.SMEM)


def dev(y, z, x, c):
    return ((y * NZ + z) * NX + x) * 2 + c


LINES_Y = [
    [dev(y, z, x, c) for y in range(NY)]
    for z in range(NZ)
    for x in range(NX)
    for c in range(2)
]
LINES_X = [
    [dev(y, z, x, c) for x in range(NX)]
    for y in range(NY)
    for z in range(NZ)
    for c in range(2)
]
COLUMNS = [
    [dev(y, z, x, c) for z in range(NZ)]
    for y in range(NY)
    for x in range(NX)
    for c in range(2)
]
SWAP = [(d, d ^ 1) for d in range(N)]


def shuffle_matrix():
    flat = np.arange(D).reshape(NY, NZ, NX, OWN)
    source = flat.transpose(0, 2, 1, 3).reshape(-1)
    matrix = np.zeros((D, D), np.float32)
    matrix[np.arange(D), source] = 1.0
    return jnp.asarray(matrix, BF)


def shift(value, steps):
    return lax.ppermute(value, "dp", [(d, (d + steps) % N) for d in range(N)])


def mm(a, b):
    return jnp.dot(a, b, preferred_element_type=F32)


def mm_t(a, b):
    return lax.dot_general(a, b, (((1,), (1,)), ((), ())), preferred_element_type=F32)


def t_mm(a, b):
    return lax.dot_general(a, b, (((0,), (0,)), ((), ())), preferred_element_type=F32)


def project(feat_ref, proj_ref, dir_ref, unit_ref, inv_ref, base=0):
    for i in range(R // BLK):
        rows = slice(i * BLK, (i + 1) * BLK)
        raw = mm(feat_ref[rows, :], proj_ref[...])
        inverse = 1.0 / jnp.sqrt(jnp.sum(raw * raw, axis=1, keepdims=True) + 1e-06)
        direction = raw * inverse
        dir_ref[rows, :] = direction
        unit_ref[base + i * BLK:base + (i + 1) * BLK, :] = direction.astype(BF)
        inv_ref[rows, :] = inverse


def turned(feat_ref, shuffle_ref, out_ref):
    out_ref[...] = mm_t(shuffle_ref[...], feat_ref[...]).astype(BF)


def raw_grad(gradient, direction, inverse):
    radial = jnp.sum(direction * gradient, axis=1, keepdims=True)
    return ((gradient - direction * radial) * inverse).astype(BF)


def first_kernel(text, image, text_proj, image_proj, shuffle,
                 dir_t, unit_t, inv_t, turn_t, dir_i, unit_i, inv_i, turn_i):
    project(text, text_proj, dir_t, unit_t, inv_t)
    project(image, image_proj, dir_i, unit_i, inv_i)
    turned(text, shuffle, turn_t)
    turned(image, shuffle, turn_i)


def second_kernel(scal, image1, image_proj, shuffle, unit_i0, unit_t0, dir_t0, inv_t0,
                  dir_i1, unit_i, inv_i1, turn_i1, grad_i, delta_t0, pair):
    scale, bias = scal[0], scal[1]
    unit_i[:R, :] = unit_i0[...]
    project(image1, image_proj, dir_i1, unit_i, inv_i1, R)
    logit = scale * mm_t(unit_i0[...], unit_t0[...]) + bias
    same = lax.broadcasted_iota(jnp.int32, (R, R), 0) == lax.broadcasted_iota(jnp.int32, (R, R), 1)
    sign = jnp.where(same, -1.0, 1.0)
    pair[:R, :] = (sign * jax.nn.sigmoid(sign * logit)).astype(BF)
    logit = scale * mm_t(unit_i[R:, :], unit_t0[...]) + bias
    pair[R:, :] = jax.nn.sigmoid(logit).astype(BF)
    grad_i[:R, :] = mm(pair[:R, :], unit_t0[...])
    grad_i[R:, :] = mm(pair[R:, :], unit_t0[...])
    delta_t0[...] = raw_grad(scale * t_mm(pair[...], unit_i[...]), dir_t0[...], inv_t0[...])
    turned(image1, shuffle, turn_i1)


def third_kernel(scal, text2, text_proj, shuffle, unit_i, dir_i0, dir_i1, inv_i0, inv_i1,
                 grad_i, delta_i, delta_t2, turn_t2, dir_t2, unit_t2, inv_t2, pair):
    scale, bias = scal[0], scal[1]
    project(text2, text_proj, dir_t2, unit_t2, inv_t2)
    for dir_i, inv_i, base in ((dir_i0, inv_i0, 0), (dir_i1, inv_i1, R)):
        rows = slice(base, base + R)
        logit = scale * mm_t(unit_i[rows, :], unit_t2[...]) + bias
        pair[rows, :] = jax.nn.sigmoid(logit).astype(BF)
        gradient = scale * (grad_i[rows, :] + mm(pair[rows, :], unit_t2[...]))
        delta_i[rows, :] = raw_grad(gradient, dir_i[...], inv_i[...])
    delta_t2[...] = raw_grad(scale * t_mm(pair[...], unit_i[...]), dir_t2[...], inv_t2[...])
    turned(text2, shuffle, turn_t2)


def term(image_core, columns, which, turn_i0, turn_i1, delta_i, turn_t0, turn_t2, delta_t0, delta_t2, put):
    @pl.when(which[0] == image_core)
    def _():
        put(mm(turn_i0[...], delta_i[:R, columns]) + mm(turn_i1[...], delta_i[R:, columns]))

    @pl.when(which[0] != image_core)
    def _():
        put(mm(turn_t0[...], delta_t0[:, columns]) + mm(turn_t2[...], delta_t2[:, columns]))


def away_kernel(columns, *refs):
    def put(value):
        refs[-1][...] = value.astype(BF)

    term(1, columns, *refs[:-1], put)


def kept_kernel(columns, back, *refs):
    def put(value):
        refs[-1][...] = (value + back[...].astype(F32)).astype(BF)

    term(0, columns, *refs[:-1], put)


def spread_kernel(columns, back, place, *refs):
    *sources, out0, out1, out2, out3, whole = refs

    def put(value):
        total = value + back[...].astype(F32)
        for k in range(NY * NX):
            whole[k] = total[k * 72:(k + 1) * 72, :]

    term(0, columns, *sources, put)
    for k, out in enumerate((out0, out1, out2, out3)):
        x = lax.rem(place[0] + k, NX)
        for y in range(NY):
            out[y] = whole[NX * y + x].astype(out.dtype)


def gather_kernel(place, own, r1, r2, r3, out0, out1, out2, out3, whole):
    whole[...] = own[...] + r1[...].astype(F32) + r2[...].astype(F32) + r3[...].astype(F32)
    for k, out in enumerate((out0, out1, out2, out3)):
        out[...] = whole[lax.rem(place[0] + k, NY)].astype(out.dtype)


def call(kernel, operands, outs, scratch=(), flops=0, name=None, grant=32):
    shapes = [jax.ShapeDtypeStruct(shape, kind) for shape, kind in outs]
    moved = sum(a.size * a.dtype.itemsize for a in operands)
    moved += sum(int(np.prod(s.shape)) * s.dtype.itemsize for s in shapes)
    return pl.pallas_call(
        kernel,
        out_shape=shapes,
        in_specs=[SMEM if a.size < 8 else VMEM for a in operands],
        out_specs=[VMEM] * len(shapes),
        scratch_shapes=[pltpu.VMEM(shape, kind) for shape, kind in scratch],
        compiler_params=pltpu.CompilerParams(vmem_limit_bytes=grant << 20),
        cost_estimate=pl.CostEstimate(flops=flops, bytes_accessed=moved, transcendentals=0),
        name=name,
    )(*operands)


def around(axis, steps):
    pairs = []
    for y in range(NY):
        for z in range(NZ):
            for x in range(NX):
                for c in range(2):
                    to = dev((y + steps) % NY, z, x, c) if axis == "y" else dev(y, z, (x + steps) % NX, c)
                    pairs.append((dev(y, z, x, c), to))
    return pairs


def local(image_feat, text_feat, image_proj, text_proj, logit_scale_logarithm, bias, counts):
    scal = jnp.stack([jnp.exp(logit_scale_logarithm[0]), bias[0]])
    rows = lax.broadcasted_iota(jnp.int32, image_feat.shape, 0)
    live = rows < counts[0] * BLK
    zero = jnp.zeros((), BF)
    text0 = jnp.where(live, text_feat, zero)
    image_feat, text0 = lax.optimization_barrier((image_feat, text0))
    image0 = jnp.where(live, image_feat, zero)
    text2 = shift(text0, 2)
    image1 = shift(image0, -1)
    shuffle = shuffle_matrix()
    me = lax.axis_index("dp")
    core = me % 2
    my_x = (me // 2 % NX).reshape(1)
    my_y = (me // (2 * NX * NZ)).reshape(1)

    unit, wide, line, turn = ((R, D), BF), ((R, D), F32), ((R, 1), F32), ((D, R), BF)
    pair = ((2 * R, R), BF)
    step = 2 * R * D * D
    dir_t0, unit_t0, inv_t0, turn_t0, dir_i0, unit_i0, inv_i0, turn_i0 = call(
        first_kernel,
        (text0, image0, text_proj, image_proj, shuffle),
        [wide, unit, line, turn] * 2,
        flops=4 * step,
        name="own_rows",
    )
    dir_i1, unit_i, inv_i1, turn_i1, grad_i, delta_t0 = call(
        second_kernel,
        (scal, image1, image_proj, shuffle, unit_i0, unit_t0, dir_t0, inv_t0),
        [wide, ((2 * R, D), BF), line, turn, ((2 * R, D), F32), unit],
        [pair],
        flops=5 * step,
        name="own_texts",
    )
    delta_i, delta_t2, turn_t2 = call(
        third_kernel,
        (scal, text2, text_proj, shuffle, unit_i, dir_i0, dir_i1, inv_i0, inv_i1, grad_i),
        [((2 * R, D), BF), unit, turn],
        [wide, unit, line, pair],
        flops=5 * step,
        name="far_texts",
        grant=36,
    )

    terms = (core.reshape(1), turn_i0, turn_i1, delta_i, turn_t0, turn_t2, delta_t0, delta_t2)
    part_a, part_b = slice(0, HALF), slice(HALF, D)
    wide_a, wide_b = HALF, D - HALF
    (away_a,) = call(functools.partial(away_kernel, part_a), terms, [((D, wide_a), BF)], flops=step, name="away_a")
    back_a = lax.ppermute(away_a, "dp", SWAP)
    (away_b,) = call(functools.partial(away_kernel, part_b), terms, [((D, wide_b), BF)], flops=step, name="away_b")
    back_b = lax.ppermute(away_b, "dp", SWAP)
    (kept_a,) = call(
        functools.partial(kept_kernel, part_a), (back_a,) + terms, [((D, wide_a), BF)], flops=step, name="kept_a"
    )
    a = lax.all_to_all(
        kept_a.reshape(NY, D // NY, wide_a), "dp", 0, 0, axis_index_groups=LINES_Y, tiled=True
    )
    kinds = (F32, BF, BF, BF)
    b = call(
        functools.partial(spread_kernel, part_b),
        (back_b, my_x) + terms,
        [((NY, 72, wide_b), kind) for kind in kinds],
        [((NY * NX, 72, wide_b), F32)],
        flops=step,
        name="kept_b",
    )
    b = [b[0]] + [lax.ppermute(b[k], "dp", around("x", k)) for k in (1, 2, 3)]
    a = jnp.sum(a.astype(F32), axis=0).astype(BF).reshape(NX, 72, wide_a)
    a = lax.all_to_all(a, "dp", 0, 0, axis_index_groups=LINES_X, tiled=True)
    b = call(
        gather_kernel,
        (my_y, *b),
        [((72, wide_b), kind) for kind in kinds],
        [((NY, 72, wide_b), F32)],
        name="sum_b",
    )
    b = [b[0]] + [lax.ppermute(b[k], "dp", around("y", k)) for k in (1, 2, 3)]
    a = jnp.sum(a.astype(F32), axis=0)
    b = b[0] + b[1].astype(F32) + b[2].astype(F32) + b[3].astype(F32)
    plane = jnp.concatenate([a, b], axis=1).astype(BF).reshape(NZ, OWN, D)
    column = lax.all_to_all(plane, "dp", 0, 0, axis_index_groups=COLUMNS, tiled=True)
    total = jnp.sum(column.astype(F32), axis=0).reshape(2, OWN * D // 2)
    first = core == 0
    mine = lax.dynamic_index_in_dim(total, core, 0, False)
    other = lax.ppermute(lax.dynamic_index_in_dim(total, 1 - core, 0, False), "dp", SWAP)
    return jnp.where(first, mine, other), jnp.where(first, other, mine)


def solution(mesh):
    return jax.shard_map(
        local,
        mesh=mesh,
        in_specs=(P("dp", None), P("dp", None), P(), P(), P(), P(), P("dp")),
        out_specs=(P("dp"), P("dp")),
        check_vma=False,
    )
```

```python
import functools

import jax
import jax.numpy as jnp
import numpy as np
from jax import lax
from jax.experimental import pallas as pl
from jax.experimental.pallas import tpu as pltpu
from jax.sharding import PartitionSpec as P

BLK = 128
D = 1152
R = 512
NY, NZ, NX = 4, 8, 4
N = 256
OWN = 9
HALF = 640
GRANTS = (10,10,12,10)
BF = jnp.bfloat16
F32 = jnp.float32
VMEM = pl.BlockSpec(memory_space=pltpu.VMEM)
SMEM = pl.BlockSpec(memory_space=pltpu.SMEM)


def dev(y, z, x, c):
    return ((y * NZ + z) * NX + x) * 2 + c


COLUMNS = [
    [dev(y, z, x, c) for z in range(NZ) for c in range(2)]
    for y in range(NY)
    for x in range(NX)
]
SWAP = [(d, d ^ 1) for d in range(N)]


def shuffle_matrix():
    flat = np.arange(D).reshape(NY, NZ, NX, OWN)
    source = flat.transpose(0, 2, 1, 3).reshape(-1)
    matrix = np.zeros((D, D), np.float32)
    matrix[np.arange(D), source] = 1.0
    return jnp.asarray(matrix, BF)


def shift(value, steps):
    return lax.ppermute(value, "dp", [(d, (d + steps) % N) for d in range(N)])


def mm(a, b):
    return jnp.dot(a, b, preferred_element_type=F32)


def mm_t(a, b):
    return lax.dot_general(a, b, (((1,), (1,)), ((), ())), preferred_element_type=F32)


def t_mm(a, b):
    return lax.dot_general(a, b, (((0,), (0,)), ((), ())), preferred_element_type=F32)


def project(feat_ref, proj_ref, dir_ref, unit_ref, inv_ref, base=0):
    for i in range(R // BLK):
        rows = slice(i * BLK, (i + 1) * BLK)
        raw = mm(feat_ref[rows, :], proj_ref[...])
        inverse = 1.0 / jnp.sqrt(jnp.sum(raw * raw, axis=1, keepdims=True) + 1e-06)
        direction = raw * inverse
        dir_ref[rows, :] = direction
        unit_ref[base + i * BLK:base + (i + 1) * BLK, :] = direction.astype(BF)
        inv_ref[rows, :] = inverse


def turned(feat_ref, shuffle_ref, out_ref):
    out_ref[...] = mm_t(shuffle_ref[...], feat_ref[...]).astype(BF)


def raw_grad(gradient, direction, inverse):
    radial = jnp.sum(direction * gradient, axis=1, keepdims=True)
    return ((gradient - direction * radial) * inverse).astype(BF)


def first_kernel(scal, text, image, text_proj, image_proj, shuffle,
                 dir_t, unit_t, inv_t, turn_t, dir_i, unit_i, inv_i, turn_i, grad_i, pair):
    scale, bias = scal[0], scal[1]
    project(text, text_proj, dir_t, unit_t, inv_t)
    project(image, image_proj, dir_i, unit_i, inv_i)
    logit = scale * mm_t(unit_i[...], unit_t[...]) + bias
    same = lax.broadcasted_iota(jnp.int32, (R, R), 0) == lax.broadcasted_iota(jnp.int32, (R, R), 1)
    sign = jnp.where(same, -1.0, 1.0)
    pair[...] = (sign * jax.nn.sigmoid(sign * logit)).astype(BF)
    grad_i[...] = mm(pair[...], unit_t[...])
    turned(text, shuffle, turn_t)
    turned(image, shuffle, turn_i)


def second_kernel(scal, image1, image_proj, shuffle, unit_i0, unit_t0, dir_t0, inv_t0, pair0,
                  dir_i1, unit_i, inv_i1, turn_i1, grad_i1, delta_t0, pair):
    scale, bias = scal[0], scal[1]
    unit_i[:R, :] = unit_i0[...]
    pair[:R, :] = pair0[...]
    project(image1, image_proj, dir_i1, unit_i, inv_i1, R)
    logit = scale * mm_t(unit_i[R:, :], unit_t0[...]) + bias
    pair[R:, :] = jax.nn.sigmoid(logit).astype(BF)
    grad_i1[...] = mm(pair[R:, :], unit_t0[...])
    delta_t0[...] = raw_grad(scale * t_mm(pair[...], unit_i[...]), dir_t0[...], inv_t0[...])
    turned(image1, shuffle, turn_i1)


def third_kernel(scal, text2, text_proj, shuffle, unit_i, dir_i0, dir_i1, inv_i0, inv_i1, grad_i0, grad_i1,
                 delta_i, delta_t2, turn_t2, dir_t2, unit_t2, inv_t2, pair):
    scale, bias = scal[0], scal[1]
    project(text2, text_proj, dir_t2, unit_t2, inv_t2)
    for dir_i, inv_i, grad_i, base in ((dir_i0, inv_i0, grad_i0, 0), (dir_i1, inv_i1, grad_i1, R)):
        rows = slice(base, base + R)
        logit = scale * mm_t(unit_i[rows, :], unit_t2[...]) + bias
        pair[rows, :] = jax.nn.sigmoid(logit).astype(BF)
        gradient = scale * (grad_i[...] + mm(pair[rows, :], unit_t2[...]))
        delta_i[rows, :] = raw_grad(gradient, dir_i[...], inv_i[...])
    delta_t2[...] = raw_grad(scale * t_mm(pair[...], unit_i[...]), dir_t2[...], inv_t2[...])
    turned(text2, shuffle, turn_t2)


def term(image_core, columns, which, turn_i0, turn_i1, delta_i, turn_t0, turn_t2, delta_t0, delta_t2, put):
    @pl.when(which[0] == image_core)
    def _():
        put(mm(turn_i0[...], delta_i[:R, columns]) + mm(turn_i1[...], delta_i[R:, columns]))

    @pl.when(which[0] != image_core)
    def _():
        put(mm(turn_t0[...], delta_t0[:, columns]) + mm(turn_t2[...], delta_t2[:, columns]))


def away_kernel(columns, *refs):
    def put(value):
        refs[-1][...] = value.astype(BF)

    term(1, columns, *refs[:-1], put)


def kept_kernel(*refs):
    *sources, out_a, out_b = refs
    for columns, out in ((slice(0, HALF), out_a), (slice(HALF, D), out_b)):
        def put(value):
            for k in range(NY * NX):
                out[k] = value[k * 72:(k + 1) * 72, :]

        term(0, columns, *sources, put)


def spread_kernel(axis, place, kept, back, out0, out1, out2, out3, whole):
    for k in range(NY * NX):
        whole[k] = kept[k] + back[k * 72:(k + 1) * 72, :].astype(F32)
    for k, out in enumerate((out0, out1, out2, out3)):
        to = lax.rem(place[0] + k, 4)
        for m in range(4):
            out[m] = whole[4 * to + m if axis == "y" else 4 * m + to].astype(out.dtype)


def gather_kernel(place, own, r1, r2, r3, out0, out1, out2, out3, whole):
    whole[...] = own[...] + r1[...].astype(F32) + r2[...].astype(F32) + r3[...].astype(F32)
    for k, out in enumerate((out0, out1, out2, out3)):
        out[...] = whole[lax.rem(place[0] + k, 4)].astype(out.dtype)


def join_kernel(a0, a1, a2, a3, b0, b1, b2, b3, out):
    a = a0[...] + a1[...].astype(F32) + a2[...].astype(F32) + a3[...].astype(F32)
    b = b0[...] + b1[...].astype(F32) + b2[...].astype(F32) + b3[...].astype(F32)
    for z in range(NZ):
        for h in range(2):
            rows = slice(OWN * z + 4 * h, OWN * z + 4 * h + 5)
            out[2 * z + h, :, :HALF] = a[rows, :].astype(BF)
            out[2 * z + h, :, HALF:] = b[rows, :].astype(BF)


def call(kernel, operands, outs, scratch=(), flops=0, name=None, grant=8):
    shapes = [jax.ShapeDtypeStruct(shape, kind) for shape, kind in outs]
    moved = sum(a.size * a.dtype.itemsize for a in operands)
    moved += sum(int(np.prod(s.shape)) * s.dtype.itemsize for s in shapes)
    return pl.pallas_call(
        kernel,
        out_shape=shapes,
        in_specs=[SMEM if a.size < 8 else VMEM for a in operands],
        out_specs=[VMEM] * len(shapes),
        scratch_shapes=[pltpu.VMEM(shape, kind) for shape, kind in scratch],
        compiler_params=pltpu.CompilerParams(vmem_limit_bytes=grant << 20),
        cost_estimate=pl.CostEstimate(flops=flops, bytes_accessed=moved, transcendentals=0),
        name=name,
    )(*operands)


def around(axis, steps):
    pairs = []
    for y in range(NY):
        for z in range(NZ):
            for x in range(NX):
                for c in range(2):
                    to = dev((y + steps) % NY, z, x, c) if axis == "y" else dev(y, z, (x + steps) % NX, c)
                    pairs.append((dev(y, z, x, c), to))
    return pairs


def local(image_feat, text_feat, image_proj, text_proj, logit_scale_logarithm, bias, counts):
    scal = jnp.stack([jnp.exp(logit_scale_logarithm[0]), bias[0]])
    rows = lax.broadcasted_iota(jnp.int32, image_feat.shape, 0)
    live = rows < counts[0] * BLK
    zero = jnp.zeros((), BF)
    text0 = jnp.where(live, text_feat, zero)
    image_feat, text0 = lax.optimization_barrier((image_feat, text0))
    image0 = jnp.where(live, image_feat, zero)
    text2 = shift(text0, 2)
    image1 = shift(image0, -1)
    shuffle = shuffle_matrix()
    me = lax.axis_index("dp")
    core = me % 2
    my_x = (me // 2 % NX).reshape(1)
    my_y = (me // (2 * NX * NZ)).reshape(1)

    unit, wide, line, turn = ((R, D), BF), ((R, D), F32), ((R, 1), F32), ((D, R), BF)
    step = 2 * R * D * D
    dir_t0, unit_t0, inv_t0, turn_t0, dir_i0, unit_i0, inv_i0, turn_i0, grad_i0, pair0 = call(
        first_kernel,
        (scal, text0, image0, text_proj, image_proj, shuffle),
        [wide, unit, line, turn] * 2 + [wide, ((R, R), BF)],
        flops=5 * step,
        name="own_rows",
        grant=GRANTS[0],
    )
    dir_i1, unit_i, inv_i1, turn_i1, grad_i1, delta_t0 = call(
        second_kernel,
        (scal, image1, image_proj, shuffle, unit_i0, unit_t0, dir_t0, inv_t0, pair0),
        [wide, ((2 * R, D), BF), line, turn, wide, unit],
        [((2 * R, R), BF)],
        flops=4 * step,
        name="own_texts",
        grant=GRANTS[1],
    )
    delta_i, delta_t2, turn_t2 = call(
        third_kernel,
        (scal, text2, text_proj, shuffle, unit_i, dir_i0, dir_i1, inv_i0, inv_i1, grad_i0, grad_i1),
        [((2 * R, D), BF), unit, turn],
        [wide, unit, line, ((2 * R, R), BF)],
        flops=5 * step,
        name="far_texts",
        grant=GRANTS[2],
    )

    terms = (core.reshape(1), turn_i0, turn_i1, delta_i, turn_t0, turn_t2, delta_t0, delta_t2)
    part_a, part_b = slice(0, HALF), slice(HALF, D)
    wide_a, wide_b = HALF, D - HALF
    (away_a,) = call(functools.partial(away_kernel, part_a), terms, [((D, wide_a), BF)], flops=step, name="away_a")
    back_a = lax.ppermute(away_a, "dp", SWAP)
    (away_b,) = call(functools.partial(away_kernel, part_b), terms, [((D, wide_b), BF)], flops=step, name="away_b")
    back_b = lax.ppermute(away_b, "dp", SWAP)
    kept_a, kept_b = call(
        kept_kernel,
        terms,
        [((16, 72, wide_a), F32), ((16, 72, wide_b), F32)],
        flops=2 * step,
        name="kept",
        grant=GRANTS[3],
    )
    kinds = (F32, BF, BF, BF)
    parts = []
    for axis, kept, back, place, width in (
        ("y", kept_a, back_a, my_y, wide_a),
        ("x", kept_b, back_b, my_x, wide_b),
    ):
        out = call(
            functools.partial(spread_kernel, axis),
            (place, kept, back),
            [((4, 72, width), kind) for kind in kinds],
            [((16, 72, width), F32)],
            name="spread_" + axis,
        )
        parts.append([out[0]] + [lax.ppermute(out[k], "dp", around(axis, k)) for k in (2, 1, 3)])
    ends = []
    for axis, part, place, width in (("x", parts[0], my_x, wide_a), ("y", parts[1], my_y, wide_b)):
        out = call(
            gather_kernel,
            (place, *part),
            [((72, width), kind) for kind in kinds],
            [((4, 72, width), F32)],
            name="sum_" + axis,
        )
        ends += [out[0]] + [lax.ppermute(out[k], "dp", around(axis, k)) for k in (2, 1, 3)]
    (plane,) = call(join_kernel, ends, [((2 * NZ, 5, D), BF)], name="join")
    column = lax.all_to_all(plane, "dp", 0, 0, axis_index_groups=COLUMNS, tiled=True)
    total = jnp.sum(column.astype(F32).reshape(NZ, 2, 5 * D), axis=0)
    mine = lax.dynamic_slice_in_dim(total, core * (D // 2), OWN * D // 2, 1)
    return mine[0], mine[1]


def solution(mesh):
    return jax.shard_map(
        local,
        mesh=mesh,
        in_specs=(P("dp", None), P("dp", None), P(), P(), P(), P(), P("dp")),
        out_specs=(P("dp"), P("dp")),
        check_vma=False,
    )
```

```python
import functools

import jax
import jax.numpy as jnp
import numpy as np
from jax import lax
from jax.experimental import pallas as pl
from jax.experimental.pallas import tpu as pltpu
from jax.sharding import PartitionSpec as P

BLK = 128
D = 1152
R = 512
NY, NZ, NX = 4, 8, 4
N = 256
OWN = 9
PART = 384
GRANTS = (10,10,12,10,10)
BF = jnp.bfloat16
F32 = jnp.float32
VMEM = pl.BlockSpec(memory_space=pltpu.VMEM)
SMEM = pl.BlockSpec(memory_space=pltpu.SMEM)


def dev(y, z, x, c):
    return ((y * NZ + z) * NX + x) * 2 + c


PLANES = [
    [dev(y, z, x, c) for y in range(NY) for x in range(NX)]
    for z in range(NZ)
    for c in range(2)
]
COLUMNS = [
    [dev(y, z, x, c) for z in range(NZ) for c in range(2)]
    for y in range(NY)
    for x in range(NX)
]
SWAP = [(d, d ^ 1) for d in range(N)]


def shuffle_matrix():
    i = lax.optimization_barrier(lax.iota(jnp.int32, D))
    group = i // OWN
    y, x, z = group // (NX * NZ), group // NZ % NX, group % NZ
    source = ((y * NZ + z) * NX + x) * OWN + i % OWN
    return (source[:, None] == lax.broadcasted_iota(jnp.int32, (D, D), 1)).astype(BF)


def shift(value, steps):
    return lax.ppermute(value, "dp", [(d, (d + steps) % N) for d in range(N)])


def mm(a, b):
    return jnp.dot(a, b, preferred_element_type=F32)


def mm_t(a, b):
    return lax.dot_general(a, b, (((1,), (1,)), ((), ())), preferred_element_type=F32)


def t_mm(a, b):
    return lax.dot_general(a, b, (((0,), (0,)), ((), ())), preferred_element_type=F32)


def project(feat_ref, proj_ref, dir_ref, unit_ref, inv_ref, base=0):
    for i in range(R // BLK):
        rows = slice(i * BLK, (i + 1) * BLK)
        raw = mm(feat_ref[rows, :], proj_ref[...])
        inverse = 1.0 / jnp.sqrt(jnp.sum(raw * raw, axis=1, keepdims=True) + 1e-06)
        direction = raw * inverse
        dir_ref[rows, :] = direction
        unit_ref[base + i * BLK:base + (i + 1) * BLK, :] = direction.astype(BF)
        inv_ref[rows, :] = inverse


def turned(feat_ref, shuffle_ref, out_ref):
    out_ref[...] = mm_t(shuffle_ref[...], feat_ref[...]).astype(BF)


def raw_grad(gradient, direction, inverse):
    radial = jnp.sum(direction * gradient, axis=1, keepdims=True)
    return ((gradient - direction * radial) * inverse).astype(BF)


def first_kernel(scal, text, image, text_proj, image_proj, shuffle,
                 dir_t, unit_t, inv_t, turn_t, dir_i, unit_i, inv_i, turn_i, grad_i, pair):
    scale, bias = scal[0], scal[1]
    project(text, text_proj, dir_t, unit_t, inv_t)
    project(image, image_proj, dir_i, unit_i, inv_i)
    logit = scale * mm_t(unit_i[...], unit_t[...]) + bias
    same = lax.broadcasted_iota(jnp.int32, (R, R), 0) == lax.broadcasted_iota(jnp.int32, (R, R), 1)
    sign = jnp.where(same, -1.0, 1.0)
    pair[...] = (sign * jax.nn.sigmoid(sign * logit)).astype(BF)
    grad_i[...] = mm(pair[...], unit_t[...])
    turned(text, shuffle, turn_t)
    turned(image, shuffle, turn_i)


def second_kernel(scal, image1, image_proj, shuffle, unit_i0, unit_t0, dir_t0, inv_t0, pair0,
                  dir_i1, unit_i, inv_i1, turn_i1, grad_i1, delta_t0, pair):
    scale, bias = scal[0], scal[1]
    unit_i[:R, :] = unit_i0[...]
    pair[:R, :] = pair0[...]
    project(image1, image_proj, dir_i1, unit_i, inv_i1, R)
    logit = scale * mm_t(unit_i[R:, :], unit_t0[...]) + bias
    pair[R:, :] = jax.nn.sigmoid(logit).astype(BF)
    grad_i1[...] = mm(pair[R:, :], unit_t0[...])
    delta_t0[...] = raw_grad(scale * t_mm(pair[...], unit_i[...]), dir_t0[...], inv_t0[...])
    turned(image1, shuffle, turn_i1)


def third_kernel(scal, text2, text_proj, shuffle, unit_i, dir_i0, dir_i1, inv_i0, inv_i1, grad_i0, grad_i1,
                 delta_i, delta_t2, turn_t2, dir_t2, unit_t2, inv_t2, pair):
    scale, bias = scal[0], scal[1]
    project(text2, text_proj, dir_t2, unit_t2, inv_t2)
    for dir_i, inv_i, grad_i, base in ((dir_i0, inv_i0, grad_i0, 0), (dir_i1, inv_i1, grad_i1, R)):
        rows = slice(base, base + R)
        logit = scale * mm_t(unit_i[rows, :], unit_t2[...]) + bias
        pair[rows, :] = jax.nn.sigmoid(logit).astype(BF)
        gradient = scale * (grad_i[...] + mm(pair[rows, :], unit_t2[...]))
        delta_i[rows, :] = raw_grad(gradient, dir_i[...], inv_i[...])
    delta_t2[...] = raw_grad(scale * t_mm(pair[...], unit_i[...]), dir_t2[...], inv_t2[...])
    turned(text2, shuffle, turn_t2)


def term_kernel(image_core, which, turn_i0, turn_i1, delta_i, turn_t0, turn_t2, delta_t0, delta_t2, out):
    def total(turn_a, turn_b, delta_a, delta_b):
        @pl.loop(0, D // PART)
        def _(i):
            rows = pl.ds(pl.multiple_of(i * PART, PART), PART)
            out[rows, :] = (
                mm(turn_a[rows, :], delta_a[...]) + mm(turn_b[rows, :], delta_b[...])
            ).astype(out.dtype)

    @pl.when(which[0] == image_core)
    def _():
        total(turn_i0, turn_i1, delta_i.at[:R], delta_i.at[R:])

    @pl.when(which[0] != image_core)
    def _():
        total(turn_t0, turn_t2, delta_t0, delta_t2)


def join_kernel(plane, out):
    total = jnp.sum(plane[...].astype(F32), axis=0)
    for z in range(NZ):
        for h in range(2):
            out[2 * z + h] = total[OWN * z + 4 * h:OWN * z + 4 * h + 5, :].astype(BF)


def call(kernel, operands, outs, scratch=(), flops=0, name=None, grant=8):
    shapes = [jax.ShapeDtypeStruct(shape, kind) for shape, kind in outs]
    moved = sum(a.size * a.dtype.itemsize for a in operands)
    moved += sum(int(np.prod(s.shape)) * s.dtype.itemsize for s in shapes)
    return pl.pallas_call(
        kernel,
        out_shape=shapes,
        in_specs=[SMEM if a.size < 8 else VMEM for a in operands],
        out_specs=[VMEM] * len(shapes),
        scratch_shapes=[pltpu.VMEM(shape, kind) for shape, kind in scratch],
        compiler_params=pltpu.CompilerParams(vmem_limit_bytes=grant << 20),
        cost_estimate=pl.CostEstimate(flops=flops, bytes_accessed=moved, transcendentals=0),
        name=name,
    )(*operands)


def local(image_feat, text_feat, image_proj, text_proj, logit_scale_logarithm, bias, counts):
    scal = jnp.stack([jnp.exp(logit_scale_logarithm[0]), bias[0]])
    rows = lax.broadcasted_iota(jnp.int32, image_feat.shape, 0)
    live = rows < counts[0] * BLK
    zero = jnp.zeros((), BF)
    text0 = jnp.where(live, text_feat, zero)
    image_feat, text0 = lax.optimization_barrier((image_feat, text0))
    image0 = jnp.where(live, image_feat, zero)
    text2 = shift(text0, 2)
    image1 = shift(image0, -1)
    shuffle = shuffle_matrix()
    me = lax.axis_index("dp")
    core = me % 2

    unit, wide, line, turn = ((R, D), BF), ((R, D), F32), ((R, 1), F32), ((D, R), BF)
    step = 2 * R * D * D
    dir_t0, unit_t0, inv_t0, turn_t0, dir_i0, unit_i0, inv_i0, turn_i0, grad_i0, pair0 = call(
        first_kernel,
        (scal, text0, image0, text_proj, image_proj, shuffle),
        [wide, unit, line, turn] * 2 + [wide, ((R, R), BF)],
        flops=5 * step,
        name="own_rows",
        grant=GRANTS[0],
    )
    dir_i1, unit_i, inv_i1, turn_i1, grad_i1, delta_t0 = call(
        second_kernel,
        (scal, image1, image_proj, shuffle, unit_i0, unit_t0, dir_t0, inv_t0, pair0),
        [wide, ((2 * R, D), BF), line, turn, wide, unit],
        [((2 * R, R), BF)],
        flops=4 * step,
        name="own_texts",
        grant=GRANTS[1],
    )
    delta_i, delta_t2, turn_t2 = call(
        third_kernel,
        (scal, text2, text_proj, shuffle, unit_i, dir_i0, dir_i1, inv_i0, inv_i1, grad_i0, grad_i1),
        [((2 * R, D), BF), unit, turn],
        [wide, unit, line, ((2 * R, R), BF)],
        flops=5 * step,
        name="far_texts",
        grant=GRANTS[2],
    )

    terms = (core.reshape(1), turn_i0, turn_i1, delta_i, turn_t0, turn_t2, delta_t0, delta_t2)
    (away,) = call(
        functools.partial(term_kernel, 1), terms, [((D, D), BF)], flops=2 * step, name="away", grant=GRANTS[3]
    )
    back = lax.ppermute(away, "dp", SWAP)
    (kept,) = call(
        functools.partial(term_kernel, 0), terms, [((D, D), F32)], flops=2 * step, name="kept", grant=GRANTS[4]
    )
    chip = (kept + back.astype(F32)).astype(BF).reshape(NY * NX, NZ * OWN, D)
    plane = lax.all_to_all(chip, "dp", 0, 0, axis_index_groups=PLANES, tiled=True)
    (plane,) = call(join_kernel, (plane,), [((2 * NZ, 5, D), BF)], name="join")
    column = lax.all_to_all(plane, "dp", 0, 0, axis_index_groups=COLUMNS, tiled=True)
    total = jnp.sum(column.astype(F32).reshape(NZ, 2, 5 * D), axis=0)
    mine = lax.dynamic_slice_in_dim(total, core * (D // 2), OWN * D // 2, 1)
    return mine[0], mine[1]


def solution(mesh):
    return jax.shard_map(
        local,
        mesh=mesh,
        in_specs=(P("dp", None), P("dp", None), P(), P(), P(), P(), P("dp")),
        out_specs=(P("dp"), P("dp")),
        check_vma=False,
    )
```

```python
import functools

import jax
import jax.numpy as jnp
import numpy as np
from jax import lax
from jax.experimental import pallas as pl
from jax.experimental.pallas import tpu as pltpu
from jax.sharding import PartitionSpec as P

BLK = 128
D = 1152
R = 512
NY, NZ, NX = 4, 8, 4
N = 256
OWN = 9
PART = 576
GRANTS = (10,10,12,10,10)
BF = jnp.bfloat16
F32 = jnp.float32
VMEM = pl.BlockSpec(memory_space=pltpu.VMEM)
ANY = pl.BlockSpec(memory_space=pl.ANY)
SMEM = pl.BlockSpec(memory_space=pltpu.SMEM)


def dev(y, z, x, c):
    return ((y * NZ + z) * NX + x) * 2 + c


PLANES = [
    [dev(y, z, x, c) for y in range(NY) for x in range(NX)]
    for z in range(NZ)
    for c in range(2)
]
COLUMNS = [
    [dev(y, z, x, c) for z in range(NZ) for c in range(2)]
    for y in range(NY)
    for x in range(NX)
]
SWAP = [(d, d ^ 1) for d in range(N)]


def shuffle_matrix():
    i = lax.optimization_barrier(lax.iota(jnp.int32, D))
    group = i // OWN
    y, x, z = group // (NX * NZ), group // NZ % NX, group % NZ
    source = ((y * NZ + z) * NX + x) * OWN + i % OWN
    return (source[:, None] == lax.broadcasted_iota(jnp.int32, (D, D), 1)).astype(BF)


def shift(value, steps):
    return lax.ppermute(value, "dp", [(d, (d + steps) % N) for d in range(N)])


def mm(a, b):
    return jnp.dot(a, b, preferred_element_type=F32)


def mm_t(a, b):
    return lax.dot_general(a, b, (((1,), (1,)), ((), ())), preferred_element_type=F32)


def t_mm(a, b):
    return lax.dot_general(a, b, (((0,), (0,)), ((), ())), preferred_element_type=F32)


def project(feat_ref, proj_ref, dir_ref, unit_ref, inv_ref, base=0):
    for i in range(R // BLK):
        rows = slice(i * BLK, (i + 1) * BLK)
        raw = mm(feat_ref[rows, :], proj_ref[...])
        inverse = 1.0 / jnp.sqrt(jnp.sum(raw * raw, axis=1, keepdims=True) + 1e-06)
        direction = raw * inverse
        dir_ref[rows, :] = direction
        unit_ref[base + i * BLK:base + (i + 1) * BLK, :] = direction.astype(BF)
        inv_ref[rows, :] = inverse


def turned(feat_ref, shuffle_ref, out_ref):
    out_ref[...] = mm_t(shuffle_ref[...], feat_ref[...]).astype(BF)


def raw_grad(gradient, direction, inverse):
    radial = jnp.sum(direction * gradient, axis=1, keepdims=True)
    return ((gradient - direction * radial) * inverse).astype(BF)


def live_kernel(count, text, image, text0, image0, zero, sem):
    zero[...] = jnp.zeros_like(zero)
    for a, (source, target) in enumerate(((text, text0), (image, image0))):
        for k in range(R // BLK):
            rows = slice(k * BLK, (k + 1) * BLK)

            @pl.when(k < count[0])
            def _():
                pltpu.make_async_copy(source.at[rows], target.at[rows], sem.at[a, k]).start()

            @pl.when(k >= count[0])
            def _():
                pltpu.make_async_copy(zero, target.at[rows], sem.at[a, k]).start()

    for a, target in enumerate((text0, image0)):
        for k in range(R // BLK):
            pltpu.make_async_copy(zero, target.at[k * BLK:(k + 1) * BLK], sem.at[a, k]).wait()


def first_kernel(scal, text, image, text_proj, image_proj, shuffle,
                 dir_t, unit_t, inv_t, turn_t, dir_i, unit_i, inv_i, turn_i, grad_i, pair):
    scale, bias = scal[0], scal[1]
    project(text, text_proj, dir_t, unit_t, inv_t)
    project(image, image_proj, dir_i, unit_i, inv_i)
    logit = scale * mm_t(unit_i[...], unit_t[...]) + bias
    same = lax.broadcasted_iota(jnp.int32, (R, R), 0) == lax.broadcasted_iota(jnp.int32, (R, R), 1)
    sign = jnp.where(same, -1.0, 1.0)
    pair[...] = (sign * jax.nn.sigmoid(sign * logit)).astype(BF)
    grad_i[...] = mm(pair[...], unit_t[...])
    turned(text, shuffle, turn_t)
    turned(image, shuffle, turn_i)


def second_kernel(scal, image1, image_proj, shuffle, unit_i0, unit_t0, dir_t0, inv_t0, pair0,
                  dir_i1, unit_i, inv_i1, turn_i1, grad_i1, delta_t0, pair):
    scale, bias = scal[0], scal[1]
    unit_i[:R, :] = unit_i0[...]
    pair[:R, :] = pair0[...]
    project(image1, image_proj, dir_i1, unit_i, inv_i1, R)
    logit = scale * mm_t(unit_i[R:, :], unit_t0[...]) + bias
    pair[R:, :] = jax.nn.sigmoid(logit).astype(BF)
    grad_i1[...] = mm(pair[R:, :], unit_t0[...])
    delta_t0[...] = raw_grad(scale * t_mm(pair[...], unit_i[...]), dir_t0[...], inv_t0[...])
    turned(image1, shuffle, turn_i1)


def third_kernel(scal, text2, text_proj, shuffle, unit_i, dir_i0, dir_i1, inv_i0, inv_i1, grad_i0, grad_i1,
                 delta_i, delta_t2, turn_t2, dir_t2, unit_t2, inv_t2, pair):
    scale, bias = scal[0], scal[1]
    project(text2, text_proj, dir_t2, unit_t2, inv_t2)
    for dir_i, inv_i, grad_i, base in ((dir_i0, inv_i0, grad_i0, 0), (dir_i1, inv_i1, grad_i1, R)):
        rows = slice(base, base + R)
        logit = scale * mm_t(unit_i[rows, :], unit_t2[...]) + bias
        pair[rows, :] = jax.nn.sigmoid(logit).astype(BF)
        gradient = scale * (grad_i[...] + mm(pair[rows, :], unit_t2[...]))
        delta_i[rows, :] = raw_grad(gradient, dir_i[...], inv_i[...])
    delta_t2[...] = raw_grad(scale * t_mm(pair[...], unit_i[...]), dir_t2[...], inv_t2[...])
    turned(text2, shuffle, turn_t2)


def term_kernel(image_core, which, turn_i0, turn_i1, delta_i, turn_t0, turn_t2, delta_t0, delta_t2, out):
    def total(turn_a, turn_b, delta_a, delta_b):
        @pl.loop(0, D // PART)
        def _(i):
            rows = pl.ds(pl.multiple_of(i * PART, PART), PART)
            out[rows, :] = (
                mm(turn_a[rows, :], delta_a[...]) + mm(turn_b[rows, :], delta_b[...])
            ).astype(out.dtype)

    @pl.when(which[0] == image_core)
    def _():
        total(turn_i0, turn_i1, delta_i.at[:R], delta_i.at[R:])

    @pl.when(which[0] != image_core)
    def _():
        total(turn_t0, turn_t2, delta_t0, delta_t2)


def join_kernel(plane, out, packed):
    total = jnp.sum(plane[...].astype(F32), axis=0)
    packed[...] = jnp.zeros_like(packed)
    for z in range(NZ):
        for h in range(2):
            k, top, middle, lane = 2 * z + h, OWN * z + 5 * h, OWN * z + 4, 512 * h
            packed[k, 0:4, 0:640] = total[top:top + 4, 0:640]
            packed[k, 4:8, 0:512] = total[top:top + 4, 640:D]
            packed[k, 4:5, 512:768] = total[middle:middle + 1, lane:lane + 256]
            packed[k, 5:6, 512:768] = total[middle:middle + 1, lane + 256:lane + 512]
            packed[k, 6:7, 512:640] = total[middle:middle + 1, lane + 512:lane + 640]
    out[...] = packed[...].astype(BF)


def call(kernel, operands, outs, scratch=(), flops=0, name=None, grant=8):
    shapes = [jax.ShapeDtypeStruct(shape, kind) for shape, kind in outs]
    moved = sum(a.size * a.dtype.itemsize for a in operands)
    moved += sum(int(np.prod(s.shape)) * s.dtype.itemsize for s in shapes)
    return pl.pallas_call(
        kernel,
        out_shape=shapes,
        in_specs=[SMEM if a.size < 8 else VMEM for a in operands],
        out_specs=[VMEM] * len(shapes),
        scratch_shapes=[pltpu.VMEM(shape, kind) for shape, kind in scratch],
        compiler_params=pltpu.CompilerParams(vmem_limit_bytes=grant << 20),
        cost_estimate=pl.CostEstimate(flops=flops, bytes_accessed=moved, transcendentals=0),
        name=name,
    )(*operands)


def local(image_feat, text_feat, image_proj, text_proj, logit_scale_logarithm, bias, counts):
    scal = jnp.stack([jnp.exp(logit_scale_logarithm[0]), bias[0]])
    text0, image0 = pl.pallas_call(
        live_kernel,
        out_shape=[jax.ShapeDtypeStruct((R, D), BF)] * 2,
        in_specs=[SMEM, ANY, ANY],
        out_specs=[ANY, ANY],
        scratch_shapes=[pltpu.VMEM((BLK, D), BF), pltpu.SemaphoreType.DMA((2, R // BLK))],
        compiler_params=pltpu.CompilerParams(vmem_limit_bytes=58 << 20),
        name="live_rows",
    )(counts, text_feat, image_feat)
    text2 = shift(text0, 2)
    image1 = shift(image0, -1)
    shuffle = shuffle_matrix()
    me = lax.axis_index("dp")
    core = me % 2

    unit, wide, line, turn = ((R, D), BF), ((R, D), F32), ((R, 1), F32), ((D, R), BF)
    step = 2 * R * D * D
    dir_t0, unit_t0, inv_t0, turn_t0, dir_i0, unit_i0, inv_i0, turn_i0, grad_i0, pair0 = call(
        first_kernel,
        (scal, text0, image0, text_proj, image_proj, shuffle),
        [wide, unit, line, turn] * 2 + [wide, ((R, R), BF)],
        flops=5 * step,
        name="own_rows",
        grant=GRANTS[0],
    )
    dir_i1, unit_i, inv_i1, turn_i1, grad_i1, delta_t0 = call(
        second_kernel,
        (scal, image1, image_proj, shuffle, unit_i0, unit_t0, dir_t0, inv_t0, pair0),
        [wide, ((2 * R, D), BF), line, turn, wide, unit],
        [((2 * R, R), BF)],
        flops=4 * step,
        name="own_texts",
        grant=GRANTS[1],
    )
    delta_i, delta_t2, turn_t2 = call(
        third_kernel,
        (scal, text2, text_proj, shuffle, unit_i, dir_i0, dir_i1, inv_i0, inv_i1, grad_i0, grad_i1),
        [((2 * R, D), BF), unit, turn],
        [wide, unit, line, ((2 * R, R), BF)],
        flops=5 * step,
        name="far_texts",
        grant=GRANTS[2],
    )

    terms = (core.reshape(1), turn_i0, turn_i1, delta_i, turn_t0, turn_t2, delta_t0, delta_t2)
    (away,) = call(
        functools.partial(term_kernel, 1), terms, [((D, D), BF)], flops=2 * step, name="away", grant=GRANTS[3]
    )
    back = lax.ppermute(away, "dp", SWAP)
    (kept,) = call(
        functools.partial(term_kernel, 0), terms, [((D, D), F32)], flops=2 * step, name="kept", grant=GRANTS[4]
    )
    chip = (kept + back.astype(F32)).astype(BF).reshape(NY * NX, NZ * OWN, D)
    plane = lax.all_to_all(chip, "dp", 0, 0, axis_index_groups=PLANES, tiled=True)
    (plane,) = call(
        join_kernel, (plane,), [((2 * NZ, 8, 768), BF)], [((2 * NZ, 8, 768), F32)], name="join"
    )
    column = lax.all_to_all(plane, "dp", 0, 0, axis_index_groups=COLUMNS, tiled=True)
    total = jnp.sum(column.astype(F32).reshape(NZ, 2, 8, 768), axis=0)
    four = jnp.concatenate([total[:, :4, :640], total[:, 4:, :512]], axis=2).reshape(2, 4 * D)
    middle = total[:, 4:7, 512:].reshape(2, 768)[:, :640]
    whole = jnp.concatenate([middle, four, middle], axis=1)
    mine = lax.dynamic_slice_in_dim(whole, jnp.where(core == 0, 640, 64), OWN * D // 2, 1)
    return mine[0], mine[1]


def solution(mesh):
    return jax.shard_map(
        local,
        mesh=mesh,
        in_specs=(P("dp", None), P("dp", None), P(), P(), P(), P(), P("dp")),
        out_specs=(P("dp"), P("dp")),
        check_vma=False,
    )
```

```python
import functools

import jax
import jax.numpy as jnp
import numpy as np
from jax import lax
from jax.experimental import pallas as pl
from jax.experimental.pallas import tpu as pltpu
from jax.sharding import PartitionSpec as P

BLK = 128
D = 1152
R = 512
NY, NZ, NX = 4, 8, 4
N = 256
OWN = 9
PART = 576
GRANTS = (10,10,12,10,10)
BF = jnp.bfloat16
F32 = jnp.float32
VMEM = pl.BlockSpec(memory_space=pltpu.VMEM)
ANY = pl.BlockSpec(memory_space=pl.ANY)
SMEM = pl.BlockSpec(memory_space=pltpu.SMEM)


def dev(y, z, x, c):
    return ((y * NZ + z) * NX + x) * 2 + c


PLANES = [
    [dev(y, z, x, c) for y in range(NY) for x in range(NX)]
    for z in range(NZ)
    for c in range(2)
]
COLUMNS = [
    [dev(y, z, x, c) for z in range(NZ) for c in range(2)]
    for y in range(NY)
    for x in range(NX)
]
SWAP = [(d, d ^ 1) for d in range(N)]


def shuffle_matrix():
    i = lax.optimization_barrier(lax.iota(jnp.int32, D))
    group = i // OWN
    y, x, z = group // (NX * NZ), group // NZ % NX, group % NZ
    source = ((y * NZ + z) * NX + x) * OWN + i % OWN
    return (source[:, None] == lax.broadcasted_iota(jnp.int32, (D, D), 1)).astype(BF)


def shift(value, steps):
    return lax.ppermute(value, "dp", [(d, (d + steps) % N) for d in range(N)])


def mm(a, b):
    return jnp.dot(a, b, preferred_element_type=F32)


def mm_t(a, b):
    return lax.dot_general(a, b, (((1,), (1,)), ((), ())), preferred_element_type=F32)


def t_mm(a, b):
    return lax.dot_general(a, b, (((0,), (0,)), ((), ())), preferred_element_type=F32)


def project(feat_ref, proj_ref, dir_ref, unit_ref, inv_ref, base=0):
    for i in range(R // BLK):
        rows = slice(i * BLK, (i + 1) * BLK)
        raw = mm(feat_ref[rows, :], proj_ref[...])
        inverse = 1.0 / jnp.sqrt(jnp.sum(raw * raw, axis=1, keepdims=True) + 1e-06)
        direction = raw * inverse
        dir_ref[rows, :] = direction
        unit_ref[base + i * BLK:base + (i + 1) * BLK, :] = direction.astype(BF)
        inv_ref[rows, :] = inverse


def turned(feat_ref, shuffle_ref, out_ref):
    out_ref[...] = mm_t(shuffle_ref[...], feat_ref[...]).astype(BF)


def raw_grad(gradient, direction, inverse):
    radial = jnp.sum(direction * gradient, axis=1, keepdims=True)
    return ((gradient - direction * radial) * inverse).astype(BF)


def live_kernel(count, text, image, text0, image0, held, sem):
    jobs = ((text, text0), (image, image0))
    blocks = [slice(k * BLK, (k + 1) * BLK) for k in range(R // BLK)]
    for a, (source, _) in enumerate(jobs):
        for k, rows in enumerate(blocks):
            @pl.when(k < count[0])
            def _():
                pltpu.make_async_copy(source.at[rows], held.at[a, rows], sem.at[0, a, k]).start()

            @pl.when(k >= count[0])
            def _():
                held[a, rows] = jnp.zeros((BLK, D), BF)

    for a, (source, target) in enumerate(jobs):
        for k, rows in enumerate(blocks):
            @pl.when(k < count[0])
            def _():
                pltpu.make_async_copy(source.at[rows], held.at[a, rows], sem.at[0, a, k]).wait()

            pltpu.make_async_copy(held.at[a, rows], target.at[rows], sem.at[1, a, k]).start()
    for a, (_, target) in enumerate(jobs):
        for k, rows in enumerate(blocks):
            pltpu.make_async_copy(held.at[a, rows], target.at[rows], sem.at[1, a, k]).wait()


def first_kernel(scal, text, image, text_proj, image_proj, shuffle,
                 dir_t, unit_t, inv_t, turn_t, dir_i, unit_i, inv_i, turn_i, grad_i, pair):
    scale, bias = scal[0], scal[1]
    project(text, text_proj, dir_t, unit_t, inv_t)
    project(image, image_proj, dir_i, unit_i, inv_i)
    logit = scale * mm_t(unit_i[...], unit_t[...]) + bias
    same = lax.broadcasted_iota(jnp.int32, (R, R), 0) == lax.broadcasted_iota(jnp.int32, (R, R), 1)
    sign = jnp.where(same, -1.0, 1.0)
    pair[...] = (sign * jax.nn.sigmoid(sign * logit)).astype(BF)
    grad_i[...] = mm(pair[...], unit_t[...])
    turned(text, shuffle, turn_t)
    turned(image, shuffle, turn_i)


def second_kernel(scal, image1, image_proj, shuffle, unit_i0, unit_t0, dir_t0, inv_t0, pair0,
                  dir_i1, unit_i, inv_i1, turn_i1, grad_i1, delta_t0, pair):
    scale, bias = scal[0], scal[1]
    unit_i[:R, :] = unit_i0[...]
    pair[:R, :] = pair0[...]
    project(image1, image_proj, dir_i1, unit_i, inv_i1, R)
    logit = scale * mm_t(unit_i[R:, :], unit_t0[...]) + bias
    pair[R:, :] = jax.nn.sigmoid(logit).astype(BF)
    grad_i1[...] = mm(pair[R:, :], unit_t0[...])
    delta_t0[...] = raw_grad(scale * t_mm(pair[...], unit_i[...]), dir_t0[...], inv_t0[...])
    turned(image1, shuffle, turn_i1)


def third_kernel(scal, text2, text_proj, shuffle, unit_i, dir_i0, dir_i1, inv_i0, inv_i1, grad_i0, grad_i1,
                 delta_i, delta_t2, turn_t2, dir_t2, unit_t2, inv_t2, pair):
    scale, bias = scal[0], scal[1]
    project(text2, text_proj, dir_t2, unit_t2, inv_t2)
    for dir_i, inv_i, grad_i, base in ((dir_i0, inv_i0, grad_i0, 0), (dir_i1, inv_i1, grad_i1, R)):
        rows = slice(base, base + R)
        logit = scale * mm_t(unit_i[rows, :], unit_t2[...]) + bias
        pair[rows, :] = jax.nn.sigmoid(logit).astype(BF)
        gradient = scale * (grad_i[...] + mm(pair[rows, :], unit_t2[...]))
        delta_i[rows, :] = raw_grad(gradient, dir_i[...], inv_i[...])
    delta_t2[...] = raw_grad(scale * t_mm(pair[...], unit_i[...]), dir_t2[...], inv_t2[...])
    turned(text2, shuffle, turn_t2)


def term_kernel(image_core, which, turn_i0, turn_i1, delta_i, turn_t0, turn_t2, delta_t0, delta_t2, out):
    def total(turn_a, turn_b, delta_a, delta_b):
        @pl.loop(0, D // PART)
        def _(i):
            rows = pl.ds(pl.multiple_of(i * PART, PART), PART)
            out[rows, :] = (
                mm(turn_a[rows, :], delta_a[...]) + mm(turn_b[rows, :], delta_b[...])
            ).astype(out.dtype)

    @pl.when(which[0] == image_core)
    def _():
        total(turn_i0, turn_i1, delta_i.at[:R], delta_i.at[R:])

    @pl.when(which[0] != image_core)
    def _():
        total(turn_t0, turn_t2, delta_t0, delta_t2)


def join_kernel(plane, out, packed):
    total = jnp.sum(plane[...].astype(F32), axis=0)
    packed[...] = jnp.zeros_like(packed)
    for z in range(NZ):
        for h in range(2):
            k, top, middle, lane = 2 * z + h, OWN * z + 5 * h, OWN * z + 4, 512 * h
            packed[k, 0:4, 0:640] = total[top:top + 4, 0:640]
            packed[k, 4:8, 0:512] = total[top:top + 4, 640:D]
            packed[k, 4:5, 512:768] = total[middle:middle + 1, lane:lane + 256]
            packed[k, 5:6, 512:768] = total[middle:middle + 1, lane + 256:lane + 512]
            packed[k, 6:7, 512:640] = total[middle:middle + 1, lane + 512:lane + 640]
    out[...] = packed[...].astype(BF)


def call(kernel, operands, outs, scratch=(), flops=0, name=None, grant=8):
    shapes = [jax.ShapeDtypeStruct(shape, kind) for shape, kind in outs]
    moved = sum(a.size * a.dtype.itemsize for a in operands)
    moved += sum(int(np.prod(s.shape)) * s.dtype.itemsize for s in shapes)
    return pl.pallas_call(
        kernel,
        out_shape=shapes,
        in_specs=[SMEM if a.size < 8 else VMEM for a in operands],
        out_specs=[VMEM] * len(shapes),
        scratch_shapes=[pltpu.VMEM(shape, kind) for shape, kind in scratch],
        compiler_params=pltpu.CompilerParams(vmem_limit_bytes=grant << 20),
        cost_estimate=pl.CostEstimate(flops=flops, bytes_accessed=moved, transcendentals=0),
        name=name,
    )(*operands)


def local(image_feat, text_feat, image_proj, text_proj, logit_scale_logarithm, bias, counts):
    scal = jnp.stack([jnp.exp(logit_scale_logarithm[0]), bias[0]])
    text0, image0 = pl.pallas_call(
        live_kernel,
        out_shape=[jax.ShapeDtypeStruct((R, D), BF)] * 2,
        in_specs=[SMEM, ANY, ANY],
        out_specs=[ANY, ANY],
        scratch_shapes=[pltpu.VMEM((2, R, D), BF), pltpu.SemaphoreType.DMA((2, 2, R // BLK))],
        compiler_params=pltpu.CompilerParams(vmem_limit_bytes=58 << 20),
        name="live_rows",
    )(counts, text_feat, image_feat)
    text2 = shift(text0, 2)
    image1 = shift(image0, -1)
    shuffle = shuffle_matrix()
    me = lax.axis_index("dp")
    core = me % 2

    unit, wide, line, turn = ((R, D), BF), ((R, D), F32), ((R, 1), F32), ((D, R), BF)
    step = 2 * R * D * D
    dir_t0, unit_t0, inv_t0, turn_t0, dir_i0, unit_i0, inv_i0, turn_i0, grad_i0, pair0 = call(
        first_kernel,
        (scal, text0, image0, text_proj, image_proj, shuffle),
        [wide, unit, line, turn] * 2 + [wide, ((R, R), BF)],
        flops=5 * step,
        name="own_rows",
        grant=GRANTS[0],
    )
    dir_i1, unit_i, inv_i1, turn_i1, grad_i1, delta_t0 = call(
        second_kernel,
        (scal, image1, image_proj, shuffle, unit_i0, unit_t0, dir_t0, inv_t0, pair0),
        [wide, ((2 * R, D), BF), line, turn, wide, unit],
        [((2 * R, R), BF)],
        flops=4 * step,
        name="own_texts",
        grant=GRANTS[1],
    )
    delta_i, delta_t2, turn_t2 = call(
        third_kernel,
        (scal, text2, text_proj, shuffle, unit_i, dir_i0, dir_i1, inv_i0, inv_i1, grad_i0, grad_i1),
        [((2 * R, D), BF), unit, turn],
        [wide, unit, line, ((2 * R, R), BF)],
        flops=5 * step,
        name="far_texts",
        grant=GRANTS[2],
    )

    terms = (core.reshape(1), turn_i0, turn_i1, delta_i, turn_t0, turn_t2, delta_t0, delta_t2)
    (away,) = call(
        functools.partial(term_kernel, 1), terms, [((D, D), BF)], flops=2 * step, name="away", grant=GRANTS[3]
    )
    back = lax.ppermute(away, "dp", SWAP)
    (kept,) = call(
        functools.partial(term_kernel, 0), terms, [((D, D), F32)], flops=2 * step, name="kept", grant=GRANTS[4]
    )
    chip = (kept + back.astype(F32)).astype(BF).reshape(NY * NX, NZ * OWN, D)
    plane = lax.all_to_all(chip, "dp", 0, 0, axis_index_groups=PLANES, tiled=True)
    (plane,) = call(
        join_kernel, (plane,), [((2 * NZ, 8, 768), BF)], [((2 * NZ, 8, 768), F32)], name="join"
    )
    column = lax.all_to_all(plane, "dp", 0, 0, axis_index_groups=COLUMNS, tiled=True)
    total = jnp.sum(column.astype(F32).reshape(NZ, 2, 8, 768), axis=0)
    four = jnp.concatenate([total[:, :4, :640], total[:, 4:, :512]], axis=2).reshape(2, 4 * D)
    middle = total[:, 4:7, 512:].reshape(2, 768)[:, :640]
    whole = jnp.concatenate([middle, four, middle], axis=1)
    mine = lax.dynamic_slice_in_dim(whole, jnp.where(core == 0, 640, 64), OWN * D // 2, 1)
    return mine[0], mine[1]


def solution(mesh):
    return jax.shard_map(
        local,
        mesh=mesh,
        in_specs=(P("dp", None), P("dp", None), P(), P(), P(), P(), P("dp")),
        out_specs=(P("dp"), P("dp")),
        check_vma=False,
    )
```

```python
import functools

import jax
import jax.numpy as jnp
import numpy as np
from jax import lax
from jax.experimental import pallas as pl
from jax.experimental.pallas import tpu as pltpu
from jax.sharding import PartitionSpec as P

BLK = 128
D = 1152
R = 512
NY, NZ, NX = 4, 8, 4
N = 256
OWN = 9
PART = 576
GRANTS = (10,10,12,10,10)
BF = jnp.bfloat16
F32 = jnp.float32
VMEM = pl.BlockSpec(memory_space=pltpu.VMEM)
ANY = pl.BlockSpec(memory_space=pl.ANY)
SMEM = pl.BlockSpec(memory_space=pltpu.SMEM)


def dev(y, z, x, c):
    return ((y * NZ + z) * NX + x) * 2 + c


PLANES = [
    [dev(y, z, x, c) for y in range(NY) for x in range(NX)]
    for z in range(NZ)
    for c in range(2)
]
COLUMNS = [
    [dev(y, z, x, c) for z in range(NZ) for c in range(2)]
    for y in range(NY)
    for x in range(NX)
]
SWAP = [(d, d ^ 1) for d in range(N)]


def shuffle_matrix():
    i = lax.optimization_barrier(lax.iota(jnp.int32, D))
    group = i // OWN
    y, x, z = group // (NX * NZ), group // NZ % NX, group % NZ
    source = ((y * NZ + z) * NX + x) * OWN + i % OWN
    return (source[:, None] == lax.broadcasted_iota(jnp.int32, (D, D), 1)).astype(BF)


def shift(value, steps):
    return lax.ppermute(value, "dp", [(d, (d + steps) % N) for d in range(N)])


def mm(a, b):
    return jnp.dot(a, b, preferred_element_type=F32)


def mm_t(a, b):
    return lax.dot_general(a, b, (((1,), (1,)), ((), ())), preferred_element_type=F32)


def t_mm(a, b):
    return lax.dot_general(a, b, (((0,), (0,)), ((), ())), preferred_element_type=F32)


def project(feat_ref, proj_ref, dir_ref, unit_ref, inv_ref, base=0):
    for i in range(R // BLK):
        rows = slice(i * BLK, (i + 1) * BLK)
        raw = mm(feat_ref[rows, :], proj_ref[...])
        inverse = 1.0 / jnp.sqrt(jnp.sum(raw * raw, axis=1, keepdims=True) + 1e-06)
        direction = raw * inverse
        dir_ref[rows, :] = direction
        unit_ref[base + i * BLK:base + (i + 1) * BLK, :] = direction.astype(BF)
        inv_ref[rows, :] = inverse


def turned(feat_ref, shuffle_ref, out_ref):
    out_ref[...] = mm_t(shuffle_ref[...], feat_ref[...]).astype(BF)


def raw_grad(gradient, direction, inverse):
    radial = jnp.sum(direction * gradient, axis=1, keepdims=True)
    return ((gradient - direction * radial) * inverse).astype(BF)


def live_kernel(count, text, image, text0, image0, held, sem):
    jobs = ((text, text0), (image, image0))
    blocks = [slice(k * BLK, (k + 1) * BLK) for k in range(R // BLK)]
    for a, (source, _) in enumerate(jobs):
        for k, rows in enumerate(blocks):
            @pl.when(k < count[0])
            def _():
                pltpu.make_async_copy(source.at[rows], held.at[a, rows], sem.at[0, a, k]).start()

            @pl.when(k >= count[0])
            def _():
                held[a, rows] = jnp.zeros((BLK, D), BF)

    for a, (source, target) in enumerate(jobs):
        for k, rows in enumerate(blocks):
            @pl.when(k < count[0])
            def _():
                pltpu.make_async_copy(source.at[rows], held.at[a, rows], sem.at[0, a, k]).wait()

            pltpu.make_async_copy(held.at[a, rows], target.at[rows], sem.at[1, a, k]).start()
    for a, (_, target) in enumerate(jobs):
        for k, rows in enumerate(blocks):
            pltpu.make_async_copy(held.at[a, rows], target.at[rows], sem.at[1, a, k]).wait()


def first_kernel(scal, text, image, text_proj, image_proj, shuffle,
                 dir_t, unit_t, inv_t, turn_t, dir_i, unit_i, inv_i, turn_i, grad_i, pair):
    scale, bias = scal[0], scal[1]
    project(text, text_proj, dir_t, unit_t, inv_t)
    project(image, image_proj, dir_i, unit_i, inv_i)
    logit = scale * mm_t(unit_i[...], unit_t[...]) + bias
    same = lax.broadcasted_iota(jnp.int32, (R, R), 0) == lax.broadcasted_iota(jnp.int32, (R, R), 1)
    sign = jnp.where(same, -1.0, 1.0)
    pair[...] = (sign * jax.nn.sigmoid(sign * logit)).astype(BF)
    grad_i[...] = mm(pair[...], unit_t[...])
    turned(text, shuffle, turn_t)
    turned(image, shuffle, turn_i)


def second_kernel(scal, image1, image_proj, shuffle, unit_i0, unit_t0, dir_t0, inv_t0, pair0,
                  dir_i1, unit_i, inv_i1, turn_i1, grad_i1, delta_t0, pair):
    scale, bias = scal[0], scal[1]
    unit_i[:R, :] = unit_i0[...]
    pair[:R, :] = pair0[...]
    project(image1, image_proj, dir_i1, unit_i, inv_i1, R)
    logit = scale * mm_t(unit_i[R:, :], unit_t0[...]) + bias
    pair[R:, :] = jax.nn.sigmoid(logit).astype(BF)
    grad_i1[...] = mm(pair[R:, :], unit_t0[...])
    delta_t0[...] = raw_grad(scale * t_mm(pair[...], unit_i[...]), dir_t0[...], inv_t0[...])
    turned(image1, shuffle, turn_i1)


def third_kernel(scal, text2, text_proj, shuffle, unit_i, dir_i0, dir_i1, inv_i0, inv_i1, grad_i0, grad_i1,
                 delta_i, delta_t2, turn_t2, dir_t2, unit_t2, inv_t2, pair):
    scale, bias = scal[0], scal[1]
    project(text2, text_proj, dir_t2, unit_t2, inv_t2)
    for dir_i, inv_i, grad_i, base in ((dir_i0, inv_i0, grad_i0, 0), (dir_i1, inv_i1, grad_i1, R)):
        rows = slice(base, base + R)
        logit = scale * mm_t(unit_i[rows, :], unit_t2[...]) + bias
        pair[rows, :] = jax.nn.sigmoid(logit).astype(BF)
        gradient = scale * (grad_i[...] + mm(pair[rows, :], unit_t2[...]))
        delta_i[rows, :] = raw_grad(gradient, dir_i[...], inv_i[...])
    delta_t2[...] = raw_grad(scale * t_mm(pair[...], unit_i[...]), dir_t2[...], inv_t2[...])
    turned(text2, shuffle, turn_t2)


def term_kernel(image_core, which, turn_i0, turn_i1, delta_i, turn_t0, turn_t2, delta_t0, delta_t2, out):
    def total(turn_a, turn_b, delta_a, delta_b):
        @pl.loop(0, D // PART)
        def _(i):
            rows = pl.ds(pl.multiple_of(i * PART, PART), PART)
            out[rows, :] = (
                mm(turn_a[rows, :], delta_a[...]) + mm(turn_b[rows, :], delta_b[...])
            ).astype(out.dtype)

    @pl.when(which[0] == image_core)
    def _():
        total(turn_i0, turn_i1, delta_i.at[:R], delta_i.at[R:])

    @pl.when(which[0] != image_core)
    def _():
        total(turn_t0, turn_t2, delta_t0, delta_t2)


def join_kernel(plane, out, packed):
    total = jnp.sum(plane[...].astype(F32), axis=0)
    packed[...] = jnp.zeros_like(packed)
    for z in range(NZ):
        for h in range(2):
            k, top, middle, lane = 2 * z + h, OWN * z + 5 * h, OWN * z + 4, 512 * h
            packed[k, 0:4, 0:640] = total[top:top + 4, 0:640]
            packed[k, 4:8, 0:512] = total[top:top + 4, 640:D]
            packed[k, 4:5, 512:768] = total[middle:middle + 1, lane:lane + 256]
            packed[k, 5:6, 512:768] = total[middle:middle + 1, lane + 256:lane + 512]
            packed[k, 6:7, 512:640] = total[middle:middle + 1, lane + 512:lane + 640]
    out[...] = packed[...].astype(BF)


def call(kernel, operands, outs, scratch=(), flops=0, name=None, grant=8):
    shapes = [jax.ShapeDtypeStruct(shape, kind) for shape, kind in outs]
    moved = sum(a.size * a.dtype.itemsize for a in operands)
    moved += sum(int(np.prod(s.shape)) * s.dtype.itemsize for s in shapes)
    return pl.pallas_call(
        kernel,
        out_shape=shapes,
        in_specs=[SMEM if a.size < 8 else VMEM for a in operands],
        out_specs=[VMEM] * len(shapes),
        scratch_shapes=[pltpu.VMEM(shape, kind) for shape, kind in scratch],
        compiler_params=pltpu.CompilerParams(vmem_limit_bytes=grant << 20),
        cost_estimate=pl.CostEstimate(flops=flops, bytes_accessed=moved, transcendentals=0),
        name=name,
    )(*operands)


def local(image_feat, text_feat, image_proj, text_proj, logit_scale_logarithm, bias, counts):
    scal = jnp.stack([jnp.exp(logit_scale_logarithm[0]), bias[0]])
    text0, image0 = pl.pallas_call(
        live_kernel,
        out_shape=[jax.ShapeDtypeStruct((R, D), BF)] * 2,
        in_specs=[SMEM, ANY, ANY],
        out_specs=[ANY, ANY],
        scratch_shapes=[pltpu.VMEM((2, R, D), BF), pltpu.SemaphoreType.DMA((2, 2, R // BLK))],
        compiler_params=pltpu.CompilerParams(vmem_limit_bytes=58 << 20),
        name="live_rows",
    )(counts, text_feat, image_feat)
    text2 = shift(text0, 2)
    shuffle = shuffle_matrix()
    image0, shuffle = lax.optimization_barrier((image0, shuffle))
    image1 = shift(image0, -1)
    me = lax.axis_index("dp")
    core = me % 2

    unit, wide, line, turn = ((R, D), BF), ((R, D), F32), ((R, 1), F32), ((D, R), BF)
    step = 2 * R * D * D
    dir_t0, unit_t0, inv_t0, turn_t0, dir_i0, unit_i0, inv_i0, turn_i0, grad_i0, pair0 = call(
        first_kernel,
        (scal, text0, image0, text_proj, image_proj, shuffle),
        [wide, unit, line, turn] * 2 + [wide, ((R, R), BF)],
        flops=5 * step,
        name="own_rows",
        grant=GRANTS[0],
    )
    dir_i1, unit_i, inv_i1, turn_i1, grad_i1, delta_t0 = call(
        second_kernel,
        (scal, image1, image_proj, shuffle, unit_i0, unit_t0, dir_t0, inv_t0, pair0),
        [wide, ((2 * R, D), BF), line, turn, wide, unit],
        [((2 * R, R), BF)],
        flops=4 * step,
        name="own_texts",
        grant=GRANTS[1],
    )
    delta_i, delta_t2, turn_t2 = call(
        third_kernel,
        (scal, text2, text_proj, shuffle, unit_i, dir_i0, dir_i1, inv_i0, inv_i1, grad_i0, grad_i1),
        [((2 * R, D), BF), unit, turn],
        [wide, unit, line, ((2 * R, R), BF)],
        flops=5 * step,
        name="far_texts",
        grant=GRANTS[2],
    )

    terms = (core.reshape(1), turn_i0, turn_i1, delta_i, turn_t0, turn_t2, delta_t0, delta_t2)
    (away,) = call(
        functools.partial(term_kernel, 1), terms, [((D, D), BF)], flops=2 * step, name="away", grant=GRANTS[3]
    )
    back = lax.ppermute(away, "dp", SWAP)
    (kept,) = call(
        functools.partial(term_kernel, 0), terms, [((D, D), F32)], flops=2 * step, name="kept", grant=GRANTS[4]
    )
    chip = (kept + back.astype(F32)).astype(BF).reshape(NY * NX, NZ * OWN, D)
    plane = lax.all_to_all(chip, "dp", 0, 0, axis_index_groups=PLANES, tiled=True)
    (plane,) = call(
        join_kernel, (plane,), [((2 * NZ, 8, 768), BF)], [((2 * NZ, 8, 768), F32)], name="join"
    )
    column = lax.all_to_all(plane, "dp", 0, 0, axis_index_groups=COLUMNS, tiled=True)
    total = jnp.sum(column.astype(F32).reshape(NZ, 2, 8, 768), axis=0)
    four = jnp.concatenate([total[:, :4, :640], total[:, 4:, :512]], axis=2).reshape(2, 4 * D)
    middle = total[:, 4:7, 512:].reshape(2, 768)[:, :640]
    whole = jnp.concatenate([middle, four, middle], axis=1)
    mine = lax.dynamic_slice_in_dim(whole, jnp.where(core == 0, 640, 64), OWN * D // 2, 1)
    return mine[0], mine[1]


def solution(mesh):
    return jax.shard_map(
        local,
        mesh=mesh,
        in_specs=(P("dp", None), P("dp", None), P(), P(), P(), P(), P("dp")),
        out_specs=(P("dp"), P("dp")),
        check_vma=False,
    )
```
